256 devices in a mesh: row: 16 (over z_lo, x, core), col: 16 (over y, z_hi).
Axes of the slice: x: 4, y: 4, z: 8 (z_hi: 4, z_lo: 2; z = z_hi * 2 + z_lo), core: 2. Of those that a mesh axis runs over, the one named last changes fastest.
Arguments:
- pair_density: bfloat16 [4096, 8192], P('col', 'row'), may hold values from -6 to 6
- scale_exp: int32 [4096], replicated, may hold values from -1 to 1
- pair_weight: int32 [4096], replicated, may hold values from 1 to 4
- resident_ids: int32 [512], replicated, may hold values from 0 to 4095, as said below
- diagonal_shift: float32 [8192], replicated, may hold values from 2 to 4
- background: float32 [8192, 8192], P('row', 'col'), as said below
Outputs:
- dielectric: float32 [8192, 8192], P('row', 'col')
- kernel: float32 [4096, 512], P(('col', 'row'))
The draws below stay inside these ranges and needn't reach their ends.
Inputs may be any that keep to these rules, and one draw needn't show every extreme that they name: `resident_ids`: 512 distinct pair indices. background is symmetric.
All inputs are finite; a program needn't handle non-finite values.
Results may differ from the reference program's by a relative error of at most 0.0003.
Values may be sent and summed in bfloat16 or wider, within the bound.
A program may use at most 64 MiB of HBM per device.

```python
import math
import jax
import jax.numpy as jnp
from jax import lax

NG = 8192
NRES = 512
SWEEPS = 2
NPAIR = 4096


def draw_background(key, part):
    normal_draw = jax.random.normal(jax.random.fold_in(key, 11), (NG, NG), jnp.float32)
    return (normal_draw + normal_draw.T) * (0.35 / math.sqrt(NG))


def draw_resident_ids(key, part):
    middle_ids = jax.random.permutation(jax.random.fold_in(key, 7), NPAIR - 2)[:NRES - 2] + 1
    chosen = jnp.concatenate([middle_ids.astype(jnp.int32), jnp.array([0, NPAIR - 1], jnp.int32)])
    shuffle = jax.random.permutation(jax.random.fold_in(key, 8), NRES)
    return chosen[shuffle].astype(jnp.int32)


def touch_ends(drawn, stream_key, least, top_value):
    extent = drawn.shape
    index_at = [jax.random.randint(jax.random.fold_in(stream_key, axis), (), 0, extent[axis]) for axis in range(len(extent))]
    drawn = drawn.at[tuple(index_at)].set(least)
    longest = extent.index(max(extent))
    index_at[longest] = (index_at[longest] + 1) % extent[longest]
    return drawn.at[tuple(index_at)].set(top_value)


def block_scale(own_key, shape, cuts, smallest, top_value):
    def one(axis_at, blocks):
        draws = jax.random.uniform(jax.random.fold_in(jax.random.fold_in(own_key, 6), axis_at), (blocks,), jnp.float32, smallest / len(cuts), top_value / len(cuts))
        return jnp.repeat(jnp.exp(draws), shape[axis_at] // blocks).reshape((-1,) + (1,) * (len(shape) - axis_at - 1))

    gain = one(*cuts[0])
    for cut in cuts[1:]:
        gain = gain * one(*cut)
    return gain


def noise(stream_key, shape, spread, bound, split=(), kind=jnp.bfloat16):
    result = jax.random.normal(stream_key, shape, jnp.float32) * spread
    if len(split) > 0:
        result = block_scale(stream_key, shape, split, -0.22, 0.18) * result
    return jnp.clip(result, min=-bound, max=bound).astype(kind)


def setup_inputs(seed: int = 0) -> dict:
    seeds = jax.random.split(jax.random.key(seed), 7)
    pair_density = noise(seeds[0], (NPAIR, NG), 1.0, 6.0, ((0, 16), (1, 16)))
    scale_exp = touch_ends(jax.random.randint(seeds[1], (NPAIR,), -1, 2), jax.random.fold_in(seeds[1], 1), -1, 1).astype(jnp.int32)
    pair_weight = touch_ends(jax.random.randint(seeds[2], (NPAIR,), 1, 5), jax.random.fold_in(seeds[2], 1), 1, 4).astype(jnp.int32)
    resident_ids = draw_resident_ids(jax.random.fold_in(seeds[6], 71), 0)
    diagonal_shift = jnp.clip(jnp.exp(jax.random.uniform(seeds[4], (NG,), jnp.float32, math.log(2.0), math.log(4.0))), 2.0, 4.0)
    background = draw_background(jax.random.fold_in(seeds[6], 71), 0)
    return dict(pair_density=pair_density, scale_exp=scale_exp, pair_weight=pair_weight, resident_ids=resident_ids, diagonal_shift=diagonal_shift, background=background)


damping = 0.5

def scale_factor(exponent):
    return jnp.where(exponent < 0, 0.5, jnp.where(exponent > 0, 2.0, 1.0)).astype(jnp.float32)

def reference(pair_density, scale_exp, pair_weight, resident_ids, diagonal_shift, background):
    factor = scale_factor(scale_exp)
    scaled = (pair_density.astype(jnp.float32) * factor[:, None]).astype(jnp.bfloat16)
    response = lax.dot_general(scaled, scaled, (((0,), (0,)), ((), ())), preferred_element_type=jnp.float32) / (4 * NPAIR)
    dielectric = background + response + jnp.diag(diagonal_shift)
    wide_scaled = scaled.astype(jnp.float32)
    precond = diagonal_shift + jnp.einsum('pg,pg->g', wide_scaled, wide_scaled) / (4 * NPAIR)
    source = pair_density[resident_ids].astype(jnp.float32).T
    screened = source / precond[:, None]
    for sweep_index in range(SWEEPS):
        image = jnp.dot(dielectric, screened, precision=lax.Precision.HIGHEST)
        screened = screened + damping * (source - image) / precond[:, None]
    product = jnp.dot(pair_density.astype(jnp.float32), screened, precision=lax.Precision.HIGHEST)
    kernel = pair_weight.astype(jnp.float32)[:, None] * product / math.sqrt(NG)
    return (dielectric, kernel)
```

```python
import math

import jax
import jax.numpy as jnp
from jax import lax
from jax.experimental import pallas as pl
from jax.experimental.pallas import tpu as pltpu
from jax.sharding import PartitionSpec as P

NG = 8192
NRES = 512
MESH = pl.DeviceIdType.MESH
BF = jnp.bfloat16
F32 = jnp.float32


class Place:
    def __init__(self):
        self.r = lax.axis_index("row")
        self.c = lax.axis_index("col")
        self.zl = self.r // 8
        self.x = (self.r // 2) % 4
        self.k = self.r % 2
        self.y = self.c // 4
        self.h = self.c % 4

    def row(self, zl=0, x=0, k=0):
        return ((self.zl + zl) % 2) * 8 + ((self.x + x) % 4) * 2 + (self.k + k) % 2

    def col(self, y=0, h=0):
        return ((self.y + y) % 4) * 4 + (self.h + h) % 4


def remote(src, dst, send, recv, row, col):
    return pltpu.make_async_remote_copy(
        src_ref=src, dst_ref=dst, send_sem=send, recv_sem=recv,
        device_id=(row, col), device_id_type=MESH,
    )


def greet(partners, me=None):
    barrier = pltpu.get_barrier_semaphore()
    for row, col in partners:
        pl.semaphore_signal(barrier, inc=1, device_id=(row, col), device_id_type=MESH)
    if me is not None:
        @pl.when(me.r != me.c)
        def _():
            pl.semaphore_signal(barrier, inc=1, device_id=(me.c, me.r), device_id_type=MESH)
    count = len(partners)
    if me is not None:
        count = count + jnp.where(me.r != me.c, 1, 0)
    pl.semaphore_wait(barrier, count)


class Ring:
    def __init__(self, send, recv, base, slots, step):
        self.send, self.recv, self.base, self.slots, self.step = send, recv, base, slots, step
        self.sent = []

    def copy(self, n, ref, d):
        one = remote(ref, ref, self.send.at[self.base + n], self.recv.at[self.base + n], *self.step(d))
        return one

    def start(self):
        for n, d in ((0, 1), (1, -1)):
            one = self.copy(n, self.slots(0), d)
            one.start()
            self.sent.append(one)

    def halves(self, d, n):
        rows = self.slots(0).shape[0] // 2
        return self.slots(d).at[pl.ds(n * rows, rows)]

    def forward(self):
        for n, d in ((0, 1), (1, -1)):
            self.copy(n, self.slots(-d), d).wait_recv()
            one = self.copy(2 + n, self.halves(-d, n), d)
            one.start()
            self.sent.append(one)

    def last(self):
        for n, d in ((0, 1), (1, -1)):
            self.copy(2 + n, self.halves(-2 * d, n), d).wait_recv()

    def drain(self):
        for one in self.sent:
            one.wait_send()


def gather_kernel(a_ref, al, ar, zs, zr, ys, yr, xs, xr, ls, lr, ks, kr, ts, tr, own_sem):
    me = Place()
    greet(
        [(me.r, me.col(h=1)), (me.r, me.col(h=-1)), (me.r, me.col(y=1)), (me.r, me.col(y=-1)),
         (me.row(x=1), me.c), (me.row(x=-1), me.c), (me.row(zl=1), me.c), (me.row(k=1), me.c)],
        me,
    )
    own = pltpu.make_async_copy(a_ref, al.at[me.c], own_sem.at[0])
    own.start()
    diag = pltpu.make_async_copy(a_ref, ar.at[me.r], own_sem.at[1])
    turn = remote(a_ref, ar.at[me.c], ts, tr, me.c, me.r)
    turned = remote(ar.at[me.r], ar.at[me.r], ts, tr, me.c, me.r)

    @pl.when(me.r == me.c)
    def _():
        diag.start()

    own.wait()
    z = Ring(zs, zr, 0, lambda d: al.at[me.col(h=d)], lambda d: (me.r, me.col(h=d)))
    z.start()
    offsets = (0, -1, 1, 2)
    yy = [
        Ring(ys, yr, 4 * n, lambda d, o=o: al.at[me.col(y=d, h=o)], lambda d: (me.r, me.col(y=d)))
        for n, o in enumerate(offsets)
    ]

    @pl.when(me.r != me.c)
    def _():
        turn.start()

    yy[0].start()

    @pl.when(me.r != me.c)
    def _():
        turned.wait_recv()

    @pl.when(me.r == me.c)
    def _():
        diag.wait()

    xx = [
        Ring(xs, xr, 4 * n, lambda d, n=n: ar.at[me.row(zl=n, x=d)], lambda d: (me.row(x=d), me.c))
        for n in range(2)
    ]
    low = remote(ar.at[me.r], ar.at[me.r], ls, lr, me.row(zl=1), me.c)
    low_in = remote(ar.at[me.row(zl=1)], ar.at[me.row(zl=1)], ls, lr, me.row(zl=1), me.c)
    low.start()
    xx[0].start()
    cores = []

    def hand(n, d):
        ref = ar.at[me.row(zl=n, x=d)]
        one = remote(ref, ref, ks.at[len(cores)], kr.at[len(cores)], me.row(k=1), me.c)
        one.start()
        there = ar.at[me.row(zl=n, x=d, k=1)]
        cores.append((one, remote(there, there, ks.at[len(cores)], kr.at[len(cores)], me.row(k=1), me.c)))

    hand(0, 0)
    yy[0].forward()
    z.forward()
    yy[1].start()
    yy[2].start()
    low_in.wait_recv()
    xx[1].start()
    hand(1, 0)
    xx[0].forward()
    hand(0, 1)
    hand(0, -1)
    z.last()
    yy[3].start()
    yy[1].forward()
    yy[2].forward()
    xx[1].forward()
    hand(1, 1)
    hand(1, -1)
    xx[0].last()
    hand(0, 2)
    yy[3].forward()
    xx[1].last()
    hand(1, 2)
    for one in yy:
        one.last()
    for one, arrived in cores:
        arrived.wait_recv()
    for one in [z, *yy, *xx]:
        one.drain()
    for one, arrived in cores:
        one.wait_send()
    low.wait_send()

    @pl.when(me.r != me.c)
    def _():
        turn.wait_send()


def gather(scaled):
    depth, width = scaled.shape
    shape = jax.ShapeDtypeStruct((16, depth, width), scaled.dtype)
    dma = pltpu.SemaphoreType.DMA
    left, right = pl.pallas_call(
        gather_kernel,
        out_shape=(shape, shape),
        in_specs=[pl.BlockSpec(memory_space=pl.ANY)],
        out_specs=(pl.BlockSpec(memory_space=pl.ANY),) * 2,
        scratch_shapes=[
            dma((4,)), dma((4,)), dma((16,)), dma((16,)), dma((8,)), dma((8,)),
            dma, dma, dma((8,)), dma((8,)), dma, dma, dma((2,)),
        ],
        compiler_params=pltpu.CompilerParams(collective_id=0, has_side_effects=True),
        cost_estimate=pl.CostEstimate(flops=0, bytes_accessed=16 << 20, transcendentals=0),
        name="gather_panels",
    )(scaled)
    return left, right


def split(value):
    high = value.astype(BF)
    return high, (value - high.astype(F32)).astype(BF)


def nn(a, b):
    return lax.dot_general(a, b, (((1,), (0,)), ((), ())), preferred_element_type=F32)


def nt(a, b):
    return lax.dot_general(a, b, (((1,), (1,)), ((), ())), preferred_element_type=F32)


def rows(start, size):
    return pl.ds(pl.multiple_of(start * size, size), size)


PEERS = [(a, b) for a in range(2) for b in range(4) if (a, b) != (0, 0)]


def sweep_kernel(
    dp, src_r, src_c, pr, pc, al, weight, out,
    dh, dl, sh, sl, u1, xbuf, wbuf, rbuf, s1, u2, ybuf, tbuf, hbuf, kp, kx, ko, kbuf, kt, fin,
    cs, cr, rs, rr, gs, gr, fs, fr, ys, yr, hs, hr, k1s, k1r, k2s, k2r, as_, ar_,
):
    me = Place()
    greet(
        [(me.row(k=1), me.c)]
        + [(me.row(zl=a, x=b), me.c) for a, b in PEERS]
        + [(me.r, (me.c + d) % 16) for d in range(1, 16)]
    )
    j = me.zl * 4 + me.x
    sent = []

    def go(one):
        one.start()
        sent.append(one)

    def peer_j(a, b):
        return ((me.zl + a) % 2) * 4 + (me.x + b) % 4

    high, low = split(dp[...])
    dh[...] = high
    dl[...] = low
    high, low = split(src_r[...].astype(F32) / pr[...])
    sh[...] = high
    sl[...] = low

    def first(k):
        at = rows(k, 256)
        u1[at, :] = nn(sh[at, :], dh[...]) + nn(sh[at, :], dl[...]) + nn(sl[at, :], dh[...])

    other = 1 - me.k
    first(other)
    swap = remote(u1.at[rows(other, 256)], xbuf, cs.at[0], cr.at[0], me.row(k=1), me.c)
    go(swap)
    first(me.k)
    swap.wait_recv()
    wbuf[...] = (u1[rows(me.k, 256), :] + xbuf[...]).reshape(8, 32, 512)
    ones = []
    for n, (a, b) in enumerate(PEERS):
        one = remote(wbuf.at[peer_j(a, b)], rbuf.at[n], rs.at[n], rr.at[n], me.row(zl=a, x=b), me.c)
        go(one)
        ones.append(one)
    total = wbuf[j]
    for n, one in enumerate(ones):
        one.wait_recv()
        total = total + rbuf[n]
    q = me.k * 8 + j
    high, low = split((0.5 * src_c[rows(q, 32), :].astype(F32) + total) / pc[...])
    s1[q, 0] = high
    s1[q, 1] = low
    for n, (a, b) in enumerate(PEERS):
        go(remote(s1.at[q], s1.at[q], gs.at[n], gr.at[n], me.row(zl=a, x=b), me.c))
    hands = []

    def hand(n, jj):
        ref = s1.at[me.k * 8 + jj]
        go(remote(ref, ref, fs.at[n], fr.at[n], me.row(k=1), me.c))
        there = s1.at[other * 8 + jj]
        hands.append(remote(there, there, fs.at[n], fr.at[n], me.row(k=1), me.c))

    hand(7, j)
    for n, (a, b) in enumerate(PEERS):
        jj = peer_j(-a, -b)
        ref = s1.at[me.k * 8 + jj]
        remote(ref, ref, gs.at[n], gr.at[n], me.row(zl=a, x=b), me.c).wait_recv()
        hand(n, jj)

    def second(k):
        sl1 = s1[pl.ds(k * 8, 8), 1].reshape(256, 512)
        sh1 = s1[pl.ds(k * 8, 8), 0].reshape(256, 512)
        u2[rows(k, 256), :] = nt(sh1, dh[...]) + nt(sh1, dl[...]) + nt(sl1, dh[...])

    second(me.k)
    for one in hands:
        one.wait_recv()
    second(other)
    ones = []
    for d in range(1, 4):
        one = remote(
            u2.at[rows((me.y + d) % 4, 128)], ybuf.at[d - 1], ys.at[d - 1], yr.at[d - 1],
            me.r, me.col(y=d),
        )
        go(one)
        ones.append(one)
    total = u2[rows(me.y, 128), :]
    for d, one in enumerate(ones):
        one.wait_recv()
        total = total + ybuf[d]
    tbuf[...] = total.reshape(4, 32, 512)
    ones = []
    for d in range(1, 4):
        one = remote(
            tbuf.at[(me.h + d) % 4], hbuf.at[d - 1], hs.at[d - 1], hr.at[d - 1], me.r, me.col(h=d)
        )
        go(one)
        ones.append(one)
    total = tbuf[me.h]
    for d, one in enumerate(ones):
        one.wait_recv()
        total = total + hbuf[d]
    high, low = split((0.5 * src_r[rows(me.c, 32), :].astype(F32) + total) / pr[...])
    both = jnp.concatenate([high, low], axis=0)

    def third(ref, k):
        for jj in range(8):
            part = nt(both, al[:, jj * 2 + k].reshape(256, 512))
            ref[jj] = part[:32] + part[32:]

    third(kp, other)
    swap = remote(kp, kx, cs.at[1], cr.at[1], me.row(k=1), me.c)
    go(swap)
    third(ko, me.k)
    swap.wait_recv()
    ko[...] += kx[...]
    ones = []
    for n, (a, b) in enumerate(PEERS):
        one = remote(ko.at[peer_j(a, b)], kbuf.at[n], k1s.at[n], k1r.at[n], me.row(zl=a, x=b), me.c)
        go(one)
        ones.append(one)
    total = ko[j]
    for n, one in enumerate(ones):
        one.wait_recv()
        total = total + kbuf[n]
    turned = jnp.concatenate([total.T, jnp.zeros((256, 96), F32)], axis=1)
    kt[...] = turned.reshape(16, 16, 128)
    fin[me.c] = kt[me.c]
    for d in range(1, 16):
        to = (me.c + d) % 16
        go(remote(kt.at[to], fin.at[me.c], as_.at[d], ar_.at[d], me.r, to))
    for d in range(1, 16):
        ref = fin.at[(me.c - d) % 16]
        remote(ref, ref, as_.at[d], ar_.at[d], me.r, (me.c + d) % 16).wait_recv()
    out[...] = jnp.concatenate([fin[n][:, :32] for n in range(16)], axis=1) * weight[...]
    for one in sent:
        one.wait_send()


def sweep(dp, src_r, src_c, pr, pc, al, weight):
    dma = pltpu.SemaphoreType.DMA
    vmem = pltpu.VMEM
    sems = []
    for n in (2, 7, 7, 8, 3, 3, 7, 7, 16):
        sems += [dma((n,)), dma((n,))]
    return pl.pallas_call(
        sweep_kernel,
        out_shape=jax.ShapeDtypeStruct((16, NRES), F32),
        in_specs=[pl.BlockSpec(memory_space=pltpu.VMEM)] * 7,
        out_specs=pl.BlockSpec(memory_space=pltpu.VMEM),
        scratch_shapes=[
            vmem((512, 512), BF), vmem((512, 512), BF), vmem((512, 512), BF), vmem((512, 512), BF),
            vmem((512, 512), F32), vmem((256, 512), F32), vmem((8, 32, 512), F32), vmem((7, 32, 512), F32),
            vmem((16, 2, 32, 512), BF), vmem((512, 512), F32), vmem((3, 128, 512), F32),
            vmem((4, 32, 512), F32), vmem((3, 32, 512), F32),
            vmem((8, 32, 256), F32), vmem((8, 32, 256), F32), vmem((8, 32, 256), F32),
            vmem((7, 32, 256), F32), vmem((16, 16, 128), F32), vmem((16, 16, 128), F32),
        ] + sems,
        compiler_params=pltpu.CompilerParams(
            collective_id=1, has_side_effects=True, vmem_limit_bytes=48 << 20
        ),
        name="sweeps",
    )(dp, src_r, src_c, pr, pc, al, weight)


def scale_factor(exponent):
    return jnp.where(exponent < 0, 0.5, jnp.where(exponent > 0, 2.0, 1.0)).astype(F32)


def shards(pair_density, scale_exp, pair_weight, resident_ids, diagonal_shift, background):
    row_index = lax.axis_index("row")
    col_index = lax.axis_index("col")
    pair_dev, row_width = pair_density.shape
    col_width = background.shape[1]
    norm_scale = 4 * pair_dev * 16
    factor = scale_factor(scale_exp)
    own_factor = lax.dynamic_slice_in_dim(factor, col_index * pair_dev, pair_dev)
    scaled = (pair_density.astype(F32) * own_factor[:, None]).astype(BF)
    left, right = gather(scaled)
    left_all = left.reshape(-1, row_width)
    right_all = right.reshape(-1, col_width)
    response = lax.dot_general(
        left_all, right_all, (((0,), (0,)), ((), ())), preferred_element_type=F32
    ) / norm_scale
    row_start = row_index * row_width
    col_start = col_index * col_width
    global_rows = row_start + lax.broadcasted_iota(jnp.int32, (row_width, col_width), 0)
    global_cols = col_start + lax.broadcasted_iota(jnp.int32, (row_width, col_width), 1)
    shift_rows = lax.dynamic_slice_in_dim(diagonal_shift, row_start, row_width)
    shift_cols = lax.dynamic_slice_in_dim(diagonal_shift, col_start, col_width)
    on_diagonal = global_rows == global_cols
    dielectric = background + response + jnp.where(on_diagonal, shift_rows[:, None], 0.0)

    def precond_of(panel, shift):
        return shift + jnp.einsum("pg,pg->g", panel, panel, preferred_element_type=F32) / norm_scale

    precond_rows = precond_of(left_all, shift_rows)
    precond_cols = precond_of(right_all, shift_cols)
    inverse = (1.0 / factor[resident_ids])[:, None]
    source_rows = (left_all[resident_ids].astype(F32) * inverse).astype(BF)
    source_cols = (right_all[resident_ids].astype(F32) * inverse).astype(BF)
    step = jnp.where(on_diagonal, precond_rows[:, None], 0.0) - 0.5 * dielectric
    start = col_index * pair_dev + row_index * 16
    weights = lax.dynamic_slice_in_dim(pair_weight, start, 16).astype(F32)
    weights = weights / lax.dynamic_slice_in_dim(factor, start, 16) / math.sqrt(NG)
    kernel = sweep(
        step, source_rows, source_cols, precond_rows[None], precond_cols[None],
        left.reshape(16, 16, 16, row_width), weights[:, None],
    )
    return (dielectric, kernel)


def solution(mesh):
    return jax.shard_map(
        shards,
        mesh=mesh,
        in_specs=(P("col", "row"), P(), P(), P(), P(), P("row", "col")),
        out_specs=(P("row", "col"), P(("col", "row"), None)),
        check_vma=False,
    )
```

```python
import math

import jax
import jax.numpy as jnp
from jax import lax
from jax.experimental import pallas as pl
from jax.experimental.pallas import tpu as pltpu
from jax.sharding import PartitionSpec as P

NG = 8192
NRES = 512
NPAIR = 4096
MESH = pl.DeviceIdType.MESH
BF = jnp.bfloat16
F32 = jnp.float32
NSEM = 192


def bit(n, at):
    return (n // 2**at) % 2


def number(b3, b2, b1, b0):
    return (b3 % 2) * 8 + (b2 % 2) * 4 + (b1 % 2) * 2 + b0 % 2


def crossed(row, col):
    return number(
        bit(row, 3) + bit(col, 3), bit(row, 2) + bit(col, 2),
        bit(row, 0) + bit(col, 1), bit(row, 1) + bit(col, 0),
    )


class Place:
    def __init__(self):
        self.r = lax.axis_index("row")
        self.c = lax.axis_index("col")
        self.zl = self.r // 8
        self.x = (self.r // 2) % 4
        self.k = self.r % 2
        self.y = self.c // 4
        self.h = self.c % 4
        self.j = self.r // 2

    def row(self, zl=0, x=0, k=0):
        return ((self.zl + zl) % 2) * 8 + ((self.x + x) % 4) * 2 + (self.k + k) % 2

    def col(self, y=0, h=0):
        return ((self.y + y) % 4) * 4 + (self.h + h) % 4


class Links:
    def __init__(self, send, recv):
        self.send, self.recv, self.used, self.sent = send, recv, 0, []

    def new(self):
        self.used += 1
        return self.used - 1

    def copy(self, n, src, dst, to):
        return pltpu.make_async_remote_copy(
            src_ref=src, dst_ref=dst, send_sem=self.send.at[n], recv_sem=self.recv.at[n],
            device_id=to, device_id_type=MESH,
        )

    def go(self, n, src, dst, to):
        one = self.copy(n, src, dst, to)
        one.start()
        self.sent.append(one)

    def arrived(self, n, ref, to):
        self.copy(n, ref, ref, to).wait_recv()

    def drain(self):
        for one in self.sent:
            one.wait_send()
        self.sent = []


class Ring:
    def __init__(self, links, slots, step):
        self.links, self.slots, self.step = links, slots, step
        self.n = [links.new() for _ in range(4)]

    def start(self):
        for n, d in ((0, 1), (1, -1)):
            self.links.go(self.n[n], self.slots(0), self.slots(0), self.step(d))

    def half(self, d, n):
        size = self.slots(0).shape[0] // 2
        return self.slots(d).at[pl.ds(n * size, size)]

    def forward(self):
        for n, d in ((0, 1), (1, -1)):
            self.links.arrived(self.n[n], self.slots(-d), self.step(d))
            self.links.go(self.n[2 + n], self.half(-d, n), self.half(-d, n), self.step(d))

    def last(self):
        for n, d in ((0, 1), (1, -1)):
            self.links.arrived(self.n[2 + n], self.half(-2 * d, n), self.step(d))


def split(value):
    high = value.astype(BF)
    return high, (value - high.astype(F32)).astype(BF)


def nn(a, b):
    return lax.dot_general(a, b, (((1,), (0,)), ((), ())), preferred_element_type=F32)


def nt(a, b):
    return lax.dot_general(a, b, (((1,), (1,)), ((), ())), preferred_element_type=F32)


def tn(a, b):
    return lax.dot_general(a, b, (((0,), (0,)), ((), ())), preferred_element_type=F32)


def rows(start, size):
    return pl.ds(pl.multiple_of(start * size, size), size)


def iota(shape, axis):
    return lax.broadcasted_iota(jnp.int32, shape, axis)


def line(ref, start, count):
    return jnp.concatenate([ref[pl.ds(start * count + n, 1), :] for n in range(count)], axis=1)


def power(exponent, down=0.5, up=2.0):
    return jnp.where(exponent < 0, down, jnp.where(exponent > 0, up, 1.0)).astype(F32)


PEERS = [(a, b) for a in range(2) for b in range(4) if (a, b) != (0, 0)]
HALVES = range(2)


def screen_kernel(
    stop, density, exps, weights, ids, shift, background, dielectric, kernel,
    al, ar, hop, bg, dv, dh, dl, acc, src, s0, idc, pre,
    u1, xbuf, wbuf, rbuf, s1, u2, ybuf, tbuf, hbuf, both, kp, kx, ko, kbuf, kt, fin,
    send, recv, local,
):
    me = Place()
    links = Links(send, recv)
    barrier = pltpu.get_barrier_semaphore()
    for d in range(1, 16):
        pl.semaphore_signal(barrier, inc=1, device_id=((me.r + d) % 16, me.c), device_id_type=MESH)
        pl.semaphore_signal(barrier, inc=1, device_id=(me.r, (me.c + d) % 16), device_id_type=MESH)
    bg_in = pltpu.make_async_copy(background, bg, local.at[0])
    bg_in.start()
    factors = line(exps, me.c, 2)
    on_diagonal = iota((256, 256), 0) == iota((256, 256), 1)
    column = jnp.sum(jnp.where(on_diagonal, power(factors), 0.0), axis=1, keepdims=True)
    own = (density[...].astype(F32) * column).astype(BF).reshape(16, 16, 512)
    al[me.c] = own
    pl.semaphore_wait(barrier, 30)

    def part(ref, slot, p):
        return ref.at[slot, pl.ds(p * 8, 8)]

    first_to = (crossed_back(me.r, me.c), me.c)
    second_to = (me.r, crossed(me.r, me.c))
    stays = first_to[0] == me.r

    def slot_of(row):
        return crossed(row, me.c)

    mine = slot_of(me.r)

    class Panel:
        def __init__(self, p):
            self.p = p
            self.hop1, self.hop2, self.low = links.new(), links.new(), links.new()
            self.rings = [
                Ring(links, lambda d, n=n: part(ar, slot_of(me.row(zl=n, x=d)), p),
                     lambda d: (me.row(x=d), me.c))
                for n in range(2)
            ]
            self.hands = []

        def copy1(self):
            return links.copy(self.hop1, part(al, me.c, self.p), hop.at[pl.ds(self.p * 8, 8)], first_to)

        def copy2(self):
            return links.copy(self.hop2, hop.at[pl.ds(self.p * 8, 8)], part(ar, me.c, self.p), second_to)

        def hand(self, n, d):
            at = links.new()
            ref = part(ar, slot_of(me.row(zl=n, x=d)), self.p)
            links.go(at, ref, ref, (me.row(k=1), me.c))
            self.hands.append((at, part(ar, slot_of(me.row(zl=n, x=d, k=1)), self.p)))

        def step1(self):
            @pl.when(jnp.logical_not(stays))
            def _():
                self.copy1().start()

            @pl.when(stays)
            def _():
                hop[pl.ds(self.p * 8, 8)] = al[me.c, pl.ds(self.p * 8, 8)]

        def step2(self):
            here = hop.at[pl.ds(self.p * 8, 8)]

            @pl.when(jnp.logical_not(stays))
            def _():
                links.arrived(self.hop1, here, first_to)

            @pl.when(me.r != 0)
            def _():
                links.copy(self.hop2, here, part(ar, me.c, self.p), second_to).start()

            @pl.when(me.r == 0)
            def _():
                ar[mine, pl.ds(self.p * 8, 8)] = hop[pl.ds(self.p * 8, 8)]

        def step3(self):
            @pl.when(me.r != 0)
            def _():
                links.arrived(self.hop2, part(ar, mine, self.p), second_to)

            there = part(ar, mine, self.p)
            links.go(self.low, there, there, (me.row(zl=1), me.c))
            self.rings[0].start()
            self.hand(0, 0)

        def step4(self):
            links.arrived(self.low, part(ar, slot_of(me.row(zl=1)), self.p), (me.row(zl=1), me.c))
            self.rings[1].start()
            self.hand(1, 0)

        def forward(self, n):
            self.rings[n].forward()
            self.hand(n, 1)
            self.hand(n, -1)

        def last(self, n):
            self.rings[n].last()
            self.hand(n, 2)

        def end(self):
            for at, ref in self.hands:
                links.arrived(at, ref, (me.row(k=1), me.c))

        def drain(self):
            @pl.when(jnp.logical_not(stays))
            def _():
                self.copy1().wait_send()

            @pl.when(me.r != 0)
            def _():
                self.copy2().wait_send()

    panel = [Panel(p) for p in range(2)]
    zz = [
        Ring(links, lambda d, p=p: part(al, me.col(h=d), p), lambda d: (me.r, me.col(h=d)))
        for p in range(2)
    ]
    yy = [
        [
            Ring(links, lambda d, p=p, o=o: part(al, me.col(y=d, h=o), p),
                 lambda d: (me.r, me.col(y=d)))
            for o in (0, -1, 1, 2)
        ]
        for p in range(2)
    ]
    panel[0].step1()
    panel[1].step1()
    zz[0].start()
    yy[0][0].start()
    zz[1].start()
    yy[1][0].start()

    to_lane = iota((512, 512), 0)
    to_lane = (to_lane % 256) // 16 * 32 + to_lane // 256 * 16 + to_lane % 16
    wanted = jnp.where(to_lane == iota((512, 512), 1), line(ids, 0, 4), 0)
    idc[...] = jnp.broadcast_to(jnp.sum(wanted, axis=1, keepdims=True), (512, 128))
    acc[...] = jnp.zeros((512, 512), F32)
    pre[...] = jnp.zeros((2, 1, 512), F32)

    def picks(id_column, slot):
        count = id_column.shape[0]
        inverse = power(line(exps, slot, 2), 2.0, 0.5)
        hit = id_column == iota((count, 256), 1) + slot * 256
        return jnp.where(hit, inverse, 0.0).astype(BF)

    def squares(n, ref, slot):
        wide = ref[slot].reshape(256, 512).astype(F32)
        pre[n] += jnp.sum(wide * wide, axis=0, keepdims=True)

    def take(slot):
        squares(0, al, slot)
        acc[...] += nn(picks(idc[:, :1], slot), al[slot].reshape(256, 512))

    panel[0].step2()
    yy[0][0].forward()
    panel[1].step2()
    yy[1][0].forward()
    zz[0].forward()
    yy[0][1].start()
    yy[0][2].start()
    take(me.c)
    panel[0].step3()
    zz[1].forward()
    yy[1][1].start()
    yy[1][2].start()
    panel[0].step4()
    panel[1].step3()
    zz[0].last()
    yy[0][3].start()
    panel[1].step4()
    panel[0].forward(0)
    zz[1].last()
    yy[1][3].start()
    take(me.col(h=1))
    take(me.col(h=-1))
    yy[0][1].forward()
    yy[0][2].forward()
    panel[0].forward(1)
    panel[1].forward(0)
    yy[1][1].forward()
    yy[1][2].forward()
    panel[0].last(0)
    panel[1].forward(1)
    take(me.col(h=2))
    take(me.col(y=1))
    take(me.col(y=-1))
    panel[0].last(1)
    yy[0][3].forward()
    panel[1].last(0)
    panel[1].last(1)
    yy[1][3].forward()
    for o in (-1, 1, 2):
        take(me.col(y=1, h=o))
        take(me.col(y=-1, h=o))
    for n, o in enumerate((0, -1, 1, 2)):
        yy[0][n].last()
        yy[1][n].last()
        take(me.col(y=2, h=o))
    for one in panel:
        one.end()

    scale = 1.0 / (4 * NPAIR)
    shift_row = line(shift, me.r, 4)
    precond = shift_row + pre[0] * scale
    pre[0] = precond
    src[...] = acc[...].astype(BF)
    high, low = split(acc[...] / precond)
    s0[0] = high
    s0[1] = low
    bg_in.wait()
    diagonal = (iota((512, 512), 0) == iota((512, 512), 1)) & (me.r == me.c)
    response = tn(al[...].reshape(NPAIR, 512), ar[...].reshape(NPAIR, 512)) * scale
    value = bg[...] + response + jnp.where(diagonal, shift_row, 0.0)
    dv[...] = value
    high, low = split(jnp.where(diagonal, precond, 0.0) - 0.5 * value)
    dh[...] = high
    dl[...] = low
    d_out = pltpu.make_async_copy(dv, dielectric, local.at[1])
    d_out.start()

    def finish():
        links.drain()
        for one in panel:
            one.drain()
        d_out.wait()

    if stop == 0:
        kernel[...] = dv[:16, :]
        finish()
        return

    other = 1 - me.k

    def peer_j(a, b):
        return ((me.zl + a) % 2) * 4 + (me.x + b) % 4

    def swap(src_ref, dst_ref):
        at = links.new()
        links.go(at, src_ref, dst_ref, (me.row(k=1), me.c))
        return lambda: links.arrived(at, dst_ref, (me.row(k=1), me.c))

    def chain(b):
        at = pl.ds(b * 256, 256)
        u1[b] = nn(s0[0, at], dh[...]) + nn(s0[0, at], dl[...]) + nn(s0[1, at], dh[...])
        waiting = swap(u1.at[b, rows(other, 128)], xbuf.at[b])
        yield 1
        waiting()
        wbuf[b] = (u1[b, rows(me.k, 128)] + xbuf[b]).reshape(8, 16, 512)
        ns = [links.new() for _ in PEERS]
        for n, (dz, dx) in enumerate(PEERS):
            links.go(ns[n], wbuf.at[b, peer_j(dz, dx)], rbuf.at[b, n], (me.row(zl=dz, x=dx), me.c))
        if b == 0:
            for slot in range(16):
                squares(1, ar, slot)
            pre[1] = line(shift, me.c, 4) + pre[1] * scale
        q = me.k * 8 + me.j
        local_source = jnp.zeros((16, 512), F32)
        id_column = idc[rows(b * 16 + q, 16), :][:, :1]
        for slot in range(16):
            local_source += nn(picks(id_column, slot), ar[slot].reshape(256, 512))
        yield 2
        total = wbuf[b, me.j]
        for n, (dz, dx) in enumerate(PEERS):
            links.arrived(ns[n], rbuf.at[b, n], (me.row(zl=dz, x=dx), me.c))
            total = total + rbuf[b, n]
        high, low = split((0.5 * local_source + total) / pre[1])
        s1[b, q, 0] = high
        s1[b, q, 1] = low
        ns = [links.new() for _ in PEERS]
        for n, (dz, dx) in enumerate(PEERS):
            links.go(ns[n], s1.at[b, q], s1.at[b, q], (me.row(zl=dz, x=dx), me.c))
        hands = []

        def hand(j):
            n = links.new()
            links.go(n, s1.at[b, me.k * 8 + j], s1.at[b, me.k * 8 + j], (me.row(k=1), me.c))
            hands.append((n, s1.at[b, other * 8 + j]))

        hand(me.j)
        yield 3
        for n, (dz, dx) in enumerate(PEERS):
            j = peer_j(-dz, -dx)
            links.arrived(ns[n], s1.at[b, me.k * 8 + j], (me.row(zl=dz, x=dx), me.c))
            hand(j)
        yield 4
        for n, ref in hands:
            links.arrived(n, ref, (me.row(k=1), me.c))
        high = s1[b, :, 0].reshape(256, 512)
        low = s1[b, :, 1].reshape(256, 512)
        u2[b] = nt(high, dh[...]) + nt(high, dl[...]) + nt(low, dh[...])
        ns = [links.new() for _ in range(3)]
        for d in range(1, 4):
            links.go(ns[d - 1], u2.at[b, rows((me.y + d) % 4, 64)], ybuf.at[b, d - 1],
                     (me.r, me.col(y=d)))
        yield 5
        total = u2[b, rows(me.y, 64)]
        for d in range(1, 4):
            links.arrived(ns[d - 1], ybuf.at[b, d - 1], (me.r, me.col(y=d)))
            total = total + ybuf[b, d - 1]
        tbuf[b] = total.reshape(4, 16, 512)
        ns = [links.new() for _ in range(3)]
        for d in range(1, 4):
            links.go(ns[d - 1], tbuf.at[b, (me.h + d) % 4], hbuf.at[b, d - 1], (me.r, me.col(h=d)))
        yield 6
        total = tbuf[b, me.h]
        for d in range(1, 4):
            links.arrived(ns[d - 1], hbuf.at[b, d - 1], (me.r, me.col(h=d)))
            total = total + hbuf[b, d - 1]
        source = src[rows(b * 16 + me.c, 16), :].astype(F32)
        high, low = split((0.5 * source + total) / pre[0])
        both[pl.ds(b * 16, 16)] = high
        both[pl.ds(32 + b * 16, 16)] = low
        yield 7

    chains = [chain(b) for b in HALVES]
    for step in range(9):
        for b in HALVES:
            if 1 <= step - b + 1 <= 7 and step - b + 1 <= stop:
                next(chains[b])
    if stop < 8:
        kernel[...] = dv[:16, :]
        finish()
        return

    def third(ref, k):
        for j in range(8):
            product = nt(both[...], al[:, j * 2 + k].reshape(256, 512))
            ref[j] = product[:32] + product[32:]

    third(kp, other)
    waiting = swap(kp, kx)
    third(ko, me.k)
    waiting()
    ko[...] += kx[...]
    ns = [links.new() for _ in PEERS]
    for n, (dz, dx) in enumerate(PEERS):
        links.go(ns[n], ko.at[peer_j(dz, dx)], kbuf.at[n], (me.row(zl=dz, x=dx), me.c))
    total = ko[me.j]
    for n, (dz, dx) in enumerate(PEERS):
        links.arrived(ns[n], kbuf.at[n], (me.row(zl=dz, x=dx), me.c))
        total = total + kbuf[n]
    if stop == 8:
        kernel[...] = dv[:16, :]
        finish()
        return
    kt[...] = jnp.concatenate([total.T, jnp.zeros((256, 96), F32)], axis=1).reshape(16, 16, 128)
    fin[me.c] = kt[me.c]
    ns = [links.new() for _ in range(16)]
    for d in range(1, 16):
        to = (me.c + d) % 16
        links.go(ns[d], kt.at[to], fin.at[me.c], (me.r, to))
    lanes = line(weights, me.c, 2).astype(F32) * power(line(exps, me.c, 2), 2.0, 0.5)
    mask = iota((16, 256), 1) == iota((16, 256), 0) + me.r * 16
    weight = jnp.sum(jnp.where(mask, lanes, 0.0), axis=1, keepdims=True) / math.sqrt(NG)
    for d in range(1, 16):
        links.arrived(ns[d], fin.at[(me.c - d) % 16], (me.r, (me.c + d) % 16))
    kernel[...] = jnp.concatenate([fin[n][:, :32] for n in range(16)], axis=1) * weight
    finish()


def crossed_back(row, col):
    return number(
        bit(row, 3) + bit(col, 3), bit(row, 2) + bit(col, 2),
        bit(row, 0) + bit(col, 0), bit(row, 1) + bit(col, 1),
    )


def screen(density, exps, weights, ids, shift, background, stop=99):
    def body(*refs):
        screen_kernel(stop, *refs)

    dma = pltpu.SemaphoreType.DMA
    vmem = pltpu.VMEM
    inside = pl.BlockSpec(memory_space=pltpu.VMEM)
    outside = pl.BlockSpec(memory_space=pl.ANY)
    return pl.pallas_call(
        body,
        out_shape=(
            jax.ShapeDtypeStruct((512, 512), F32),
            jax.ShapeDtypeStruct((16, NRES), F32),
        ),
        in_specs=[inside] * 5 + [outside],
        out_specs=(outside, inside),
        scratch_shapes=[
            vmem((16, 16, 16, 512), BF), vmem((16, 16, 16, 512), BF), vmem((16, 16, 512), BF),
            vmem((512, 512), F32), vmem((512, 512), F32), vmem((512, 512), BF), vmem((512, 512), BF),
            vmem((512, 512), F32), vmem((512, 512), BF), vmem((2, 512, 512), BF),
            vmem((512, 128), jnp.int32), vmem((2, 1, 512), F32),
            vmem((2, 256, 512), F32), vmem((2, 128, 512), F32), vmem((2, 8, 16, 512), F32),
            vmem((2, 7, 16, 512), F32), vmem((2, 16, 2, 16, 512), BF), vmem((2, 256, 512), F32),
            vmem((2, 3, 64, 512), F32), vmem((2, 4, 16, 512), F32), vmem((2, 3, 16, 512), F32),
            vmem((64, 512), BF),
            vmem((8, 32, 256), F32), vmem((8, 32, 256), F32), vmem((8, 32, 256), F32),
            vmem((7, 32, 256), F32), vmem((16, 16, 128), F32), vmem((16, 16, 128), F32),
            dma((NSEM,)), dma((NSEM,)), dma((2,)),
        ],
        compiler_params=pltpu.CompilerParams(
            collective_id=0, has_side_effects=True, vmem_limit_bytes=56 << 20
        ),
        name="screen",
    )(density, exps, weights, ids, shift, background)


def shards(pair_density, scale_exp, pair_weight, resident_ids, diagonal_shift, background):
    return screen(
        pair_density, scale_exp.reshape(32, 128), pair_weight.reshape(32, 128),
        resident_ids.reshape(4, 128), diagonal_shift.reshape(64, 128), background,
    )


def solution(mesh):
    return jax.shard_map(
        shards,
        mesh=mesh,
        in_specs=(P("col", "row"), P(), P(), P(), P(), P("row", "col")),
        out_specs=(P("row", "col"), P(("col", "row"), None)),
        check_vma=False,
    )
```

```python
import math

import jax
import jax.numpy as jnp
from jax import lax
from jax.experimental import pallas as pl
from jax.experimental.pallas import tpu as pltpu
from jax.sharding import PartitionSpec as P

NG = 8192
NRES = 512
NPAIR = 4096
MESH = pl.DeviceIdType.MESH
BF = jnp.bfloat16
F32 = jnp.float32
NSEM = 192


def bit(n, at):
    return (n // 2**at) % 2


def number(b3, b2, b1, b0):
    return (b3 % 2) * 8 + (b2 % 2) * 4 + (b1 % 2) * 2 + b0 % 2


def crossed(row, col):
    return number(
        bit(row, 3) + bit(col, 3), bit(row, 2) + bit(col, 2),
        bit(row, 0) + bit(col, 1), bit(row, 1) + bit(col, 0),
    )


class Place:
    def __init__(self):
        self.r = lax.axis_index("row")
        self.c = lax.axis_index("col")
        self.zl = self.r // 8
        self.x = (self.r // 2) % 4
        self.k = self.r % 2
        self.y = self.c // 4
        self.h = self.c % 4
        self.j = self.r // 2

    def row(self, zl=0, x=0, k=0):
        return ((self.zl + zl) % 2) * 8 + ((self.x + x) % 4) * 2 + (self.k + k) % 2

    def col(self, y=0, h=0):
        return ((self.y + y) % 4) * 4 + (self.h + h) % 4


class Links:
    def __init__(self, send, recv):
        self.send, self.recv, self.used, self.sent = send, recv, 0, []

    def new(self):
        self.used += 1
        return self.used - 1

    def copy(self, n, src, dst, to):
        return pltpu.make_async_remote_copy(
            src_ref=src, dst_ref=dst, send_sem=self.send.at[n], recv_sem=self.recv.at[n],
            device_id=to, device_id_type=MESH,
        )

    def go(self, n, src, dst, to):
        one = self.copy(n, src, dst, to)
        one.start()
        self.sent.append(one)

    def arrived(self, n, ref, to):
        self.copy(n, ref, ref, to).wait_recv()

    def drain(self):
        for one in self.sent:
            one.wait_send()
        self.sent = []


class Ring:
    def __init__(self, links, slots, step):
        self.links, self.slots, self.step = links, slots, step
        self.n = [links.new() for _ in range(4)]

    def start(self):
        for n, d in ((0, 1), (1, -1)):
            self.links.go(self.n[n], self.slots(0), self.slots(0), self.step(d))

    def half(self, d, n):
        size = self.slots(0).shape[0] // 2
        return self.slots(d).at[pl.ds(n * size, size)]

    def forward(self):
        for n, d in ((0, 1), (1, -1)):
            self.links.arrived(self.n[n], self.slots(-d), self.step(d))
            self.links.go(self.n[2 + n], self.half(-d, n), self.half(-d, n), self.step(d))

    def last(self):
        for n, d in ((0, 1), (1, -1)):
            self.links.arrived(self.n[2 + n], self.half(-2 * d, n), self.step(d))


def split(value):
    high = value.astype(BF)
    return high, (value - high.astype(F32)).astype(BF)


def nn(a, b):
    return lax.dot_general(a, b, (((1,), (0,)), ((), ())), preferred_element_type=F32)


def nt(a, b):
    return lax.dot_general(a, b, (((1,), (1,)), ((), ())), preferred_element_type=F32)


def tn(a, b):
    return lax.dot_general(a, b, (((0,), (0,)), ((), ())), preferred_element_type=F32)


def rows(start, size):
    return pl.ds(pl.multiple_of(start * size, size), size)


def iota(shape, axis):
    return lax.broadcasted_iota(jnp.int32, shape, axis)


def line(ref, start, count):
    return jnp.concatenate([ref[pl.ds(start * count + n, 1), :] for n in range(count)], axis=1)


def power(exponent, down=0.5, up=2.0):
    return jnp.where(exponent < 0, down, jnp.where(exponent > 0, up, 1.0)).astype(F32)


PEERS = [(a, b) for a in range(2) for b in range(4) if (a, b) != (0, 0)]
HALVES = range(2)


def screen_kernel(
    stop, density, exps, weights, ids, shift, background, dielectric, kernel,
    al, ar, hop, bg, dv, dh, dl, acc, acc_c, src, s0, idc, pre,
    u1, xbuf, wbuf, rbuf, s1, u2, ybuf, tbuf, hbuf, both, kp, kx, ko, kbuf, kt, fin,
    send, recv, local,
):
    me = Place()
    links = Links(send, recv)
    barrier = pltpu.get_barrier_semaphore()
    comes_from = (crossed(me.r, me.c), me.c)
    goes_to = (crossed_back(me.r, me.c), me.c)
    second = (me.r, crossed(me.r, me.c))
    neighbours = [
        (me.row(k=1), me.c), (me.row(x=1), me.c), (me.row(x=-1), me.c), (me.row(zl=1), me.c),
        (me.r, me.col(y=1)), (me.r, me.col(y=-1)), (me.r, me.col(h=1)), (me.r, me.col(h=-1)),
    ]
    for to in neighbours:
        pl.semaphore_signal(barrier, inc=1, device_id=to, device_id_type=MESH)

    @pl.when(comes_from[0] != me.r)
    def _():
        pl.semaphore_signal(barrier, inc=1, device_id=comes_from, device_id_type=MESH)

    @pl.when(second[1] != me.c)
    def _():
        pl.semaphore_signal(barrier, inc=1, device_id=second, device_id_type=MESH)

    expected = len(neighbours) + jnp.where(goes_to[0] != me.r, 1, 0) + jnp.where(second[1] != me.c, 1, 0)
    bg_in = pltpu.make_async_copy(background, bg, local.at[0])
    bg_in.start()
    factors = line(exps, me.c, 2)
    on_diagonal = iota((256, 256), 0) == iota((256, 256), 1)
    column = jnp.sum(jnp.where(on_diagonal, power(factors), 0.0), axis=1, keepdims=True)
    own = (density[...].astype(F32) * column).astype(BF).reshape(16, 16, 512)
    al[me.c] = own
    pl.semaphore_wait(barrier, expected)

    def part(ref, slot, p):
        return ref.at[slot, pl.ds(p * 8, 8)]

    def columns(p):
        return pl.ds(p * 256, 256)

    def side(ref, slot, p):
        return ref.at[slot, :, :, columns(p)]

    first_to = (crossed_back(me.r, me.c), me.c)
    second_to = (me.r, crossed(me.r, me.c))
    stays = first_to[0] == me.r

    def slot_of(row):
        return crossed(row, me.c)

    mine = slot_of(me.r)

    class Panel:
        def __init__(self, p):
            self.p = p
            self.hop1, self.hop2, self.low = links.new(), links.new(), links.new()
            self.rings = [
                Ring(links, lambda d, n=n: side(ar, slot_of(me.row(zl=n, x=d)), p),
                     lambda d: (me.row(x=d), me.c))
                for n in range(2)
            ]
            self.hands = []

        def copy1(self):
            return links.copy(self.hop1, side(al, me.c, self.p), hop.at[:, :, columns(self.p)], first_to)

        def copy2(self):
            return links.copy(self.hop2, hop.at[:, :, columns(self.p)], side(ar, me.c, self.p), second_to)

        def hand(self, n, d):
            at = links.new()
            ref = side(ar, slot_of(me.row(zl=n, x=d)), self.p)
            links.go(at, ref, ref, (me.row(k=1), me.c))
            self.hands.append((at, side(ar, slot_of(me.row(zl=n, x=d, k=1)), self.p)))

        def step1(self):
            @pl.when(jnp.logical_not(stays))
            def _():
                self.copy1().start()

            @pl.when(stays)
            def _():
                hop[:, :, columns(self.p)] = al[me.c, :, :, columns(self.p)]

        def step2(self):
            here = hop.at[:, :, columns(self.p)]

            @pl.when(jnp.logical_not(stays))
            def _():
                links.arrived(self.hop1, here, first_to)

            @pl.when(me.r != 0)
            def _():
                links.copy(self.hop2, here, side(ar, me.c, self.p), second_to).start()

            @pl.when(me.r == 0)
            def _():
                ar[mine, :, :, columns(self.p)] = hop[:, :, columns(self.p)]

        def step3(self):
            @pl.when(me.r != 0)
            def _():
                links.arrived(self.hop2, side(ar, mine, self.p), second_to)

            there = side(ar, mine, self.p)
            links.go(self.low, there, there, (me.row(zl=1), me.c))
            self.rings[0].start()
            self.hand(0, 0)

        def step4(self):
            links.arrived(self.low, side(ar, slot_of(me.row(zl=1)), self.p), (me.row(zl=1), me.c))
            self.rings[1].start()
            self.hand(1, 0)

        def forward(self, n):
            self.rings[n].forward()
            self.hand(n, 1)
            self.hand(n, -1)

        def last(self, n):
            self.rings[n].last()
            self.hand(n, 2)

        def end(self):
            for at, ref in self.hands:
                links.arrived(at, ref, (me.row(k=1), me.c))

        def drain(self):
            @pl.when(jnp.logical_not(stays))
            def _():
                self.copy1().wait_send()

            @pl.when(me.r != 0)
            def _():
                self.copy2().wait_send()

    panel = [Panel(p) for p in range(2)]
    zz = [
        Ring(links, lambda d, p=p: part(al, me.col(h=d), p), lambda d: (me.r, me.col(h=d)))
        for p in range(2)
    ]
    yy = [
        [
            Ring(links, lambda d, p=p, o=o: part(al, me.col(y=d, h=o), p),
                 lambda d: (me.r, me.col(y=d)))
            for o in (0, -1, 1, 2)
        ]
        for p in range(2)
    ]
    panel[0].step1()
    panel[1].step1()
    zz[0].start()
    yy[0][0].start()
    zz[1].start()
    yy[1][0].start()

    to_lane = iota((512, 512), 0)
    to_lane = (to_lane % 256) // 16 * 32 + to_lane // 256 * 16 + to_lane % 16
    wanted = jnp.where(to_lane == iota((512, 512), 1), line(ids, 0, 4), 0)
    idc[...] = jnp.broadcast_to(jnp.sum(wanted, axis=1, keepdims=True), (512, 128))
    acc[...] = jnp.zeros((512, 512), F32)
    pre[...] = jnp.zeros((2, 1, 512), F32)

    def picks(id_column, slot):
        count = id_column.shape[0]
        inverse = power(line(exps, slot, 2), 2.0, 0.5)
        hit = id_column == iota((count, 256), 1) + slot * 256
        return jnp.where(hit, inverse, 0.0).astype(BF)

    def squares(value):
        wide = value.astype(F32)
        return jnp.sum(wide * wide, axis=0, keepdims=True)

    def take(slot):
        pre[0] += squares(al[slot].reshape(256, 512))
        acc[...] += nn(picks(idc[:, :1], slot), al[slot].reshape(256, 512))

    q = me.k * 8 + me.j
    own_ids = idc[rows(q, 32), :][:, :1]
    acc_c[...] = jnp.zeros((32, 512), F32)

    def take_right(p, n, d, k):
        slot = slot_of(me.row(zl=n, x=d, k=k))
        value = ar[slot, :, :, columns(p)].reshape(256, 256)
        pre[1, :, columns(p)] += squares(value)
        acc_c[:, columns(p)] += nn(picks(own_ids, slot), value)

    panel[0].step2()
    yy[0][0].forward()
    panel[1].step2()
    yy[1][0].forward()
    zz[0].forward()
    yy[0][1].start()
    yy[0][2].start()
    take(me.c)
    zz[1].forward()
    yy[1][1].start()
    yy[1][2].start()
    panel[0].step3()
    zz[0].last()
    yy[0][3].start()
    panel[0].step4()
    yy[0][1].forward()
    yy[0][2].forward()
    panel[1].step3()
    zz[1].last()
    yy[1][3].start()
    panel[0].forward(0)
    panel[1].step4()
    yy[1][1].forward()
    yy[1][2].forward()
    take(me.col(h=1))
    take(me.col(h=-1))
    panel[0].forward(1)
    panel[1].forward(0)
    take(me.col(h=2))
    panel[0].last(0)
    yy[0][3].forward()
    panel[1].forward(1)
    take(me.col(y=1))
    take(me.col(y=-1))
    panel[0].last(1)
    panel[1].last(0)
    yy[1][3].forward()
    for o in (-1, 1, 2):
        take(me.col(y=1, h=o))
        take(me.col(y=-1, h=o))
    for n in range(2):
        for d in range(4):
            take_right(0, n, d, 0)
    for n, o in enumerate((0, -1, 1, 2)):
        yy[0][n].last()
        yy[1][n].last()
        take(me.col(y=2, h=o))
    panel[1].last(1)

    scale = 1.0 / (4 * NPAIR)
    shift_row = line(shift, me.r, 4)
    precond = shift_row + pre[0] * scale
    pre[0] = precond
    src[...] = acc[...].astype(BF)
    high, low = split(acc[...] / precond)
    s0[0] = high
    s0[1] = low
    bg_in.wait()
    on_line = me.r == me.c
    d_out = pltpu.make_async_copy(dv, dielectric, local.at[1])

    def block(p):
        diagonal = (iota((512, 256), 0) == iota((512, 256), 1) + p * 256) & on_line
        right = ar[:, :, :, columns(p)].reshape(NPAIR, 256)
        response = tn(al[...].reshape(NPAIR, 512), right) * scale
        at = slice(p * 256, p * 256 + 256)
        value = bg[:, columns(p)] + response + jnp.where(diagonal, shift_row[:, at], 0.0)
        dv[:, columns(p)] = value
        high, low = split(jnp.where(diagonal, precond[:, at], 0.0) - 0.5 * value)
        dh[:, columns(p)] = high
        dl[:, columns(p)] = low

    def finish():
        links.drain()
        for one in panel:
            one.drain()
        d_out.wait()

    other = 1 - me.k

    def peer_j(a, b):
        return ((me.zl + a) % 2) * 4 + (me.x + b) % 4

    def swap(src_ref, dst_ref):
        at = links.new()
        links.go(at, src_ref, dst_ref, (me.row(k=1), me.c))
        return lambda: links.arrived(at, dst_ref, (me.row(k=1), me.c))

    def first(p):
        panel[p].end()
        block(p)
        if p == 1:
            d_out.start()
        high, low = dh[:, columns(p)], dl[:, columns(p)]
        u1[p] = nn(s0[0], high) + nn(s0[0], low) + nn(s0[1], high)
        waiting = swap(u1.at[p, rows(other, 256)], xbuf.at[p])
        yield
        if p == 1:
            for n in range(2):
                for d in range(4):
                    take_right(1, n, d, 0)
        for n in range(2):
            for d in range(4):
                take_right(p, n, d, 1)
        at = slice(p * 256, p * 256 + 256)
        precond_c = line(shift, me.c, 4)[:, at] + pre[1, :, columns(p)] * scale
        yield
        waiting()
        wbuf[p] = (u1[p, rows(me.k, 256)] + xbuf[p]).reshape(8, 32, 256)
        ns = [links.new() for _ in PEERS]
        for n, (dz, dx) in enumerate(PEERS):
            links.go(ns[n], wbuf.at[p, peer_j(dz, dx)], rbuf.at[p, n], (me.row(zl=dz, x=dx), me.c))
        yield
        total = wbuf[p, me.j]
        for n, (dz, dx) in enumerate(PEERS):
            links.arrived(ns[n], rbuf.at[p, n], (me.row(zl=dz, x=dx), me.c))
            total = total + rbuf[p, n]
        high, low = split((0.5 * acc_c[:, columns(p)] + total) / precond_c)
        s1[p, q, 0] = high
        s1[p, q, 1] = low
        ns = [links.new() for _ in PEERS]
        for n, (dz, dx) in enumerate(PEERS):
            links.go(ns[n], s1.at[p, q], s1.at[p, q], (me.row(zl=dz, x=dx), me.c))
        hands = []

        def hand(j):
            n = links.new()
            links.go(n, s1.at[p, me.k * 8 + j], s1.at[p, me.k * 8 + j], (me.row(k=1), me.c))
            hands.append((n, s1.at[p, other * 8 + j]))

        hand(me.j)
        yield
        for n, (dz, dx) in enumerate(PEERS):
            j = peer_j(-dz, -dx)
            links.arrived(ns[n], s1.at[p, me.k * 8 + j], (me.row(zl=dz, x=dx), me.c))
            hand(j)
        yield
        for n, ref in hands:
            links.arrived(n, ref, (me.row(k=1), me.c))
        yield

    def product(b, p):
        high = s1[p, pl.ds(b * 8, 8), 0].reshape(256, 256)
        low = s1[p, pl.ds(b * 8, 8), 1].reshape(256, 256)
        dhp, dlp = dh[:, columns(p)], dl[:, columns(p)]
        return nt(high, dhp) + nt(high, dlp) + nt(low, dhp)

    ones = [first(p) for p in range(2)]
    for p in (0, 0, 0, 1, 0, 1, 1, 0, 1, 0):
        next(ones[p])
    for b in HALVES:
        u2[b] = product(b, 0)
    for p in (1, 1):
        next(ones[p])

    def chain(b):
        u2[b] += product(b, 1)
        ns = [links.new() for _ in range(3)]
        for d in range(1, 4):
            links.go(ns[d - 1], u2.at[b, rows((me.y + d) % 4, 64)], ybuf.at[b, d - 1],
                     (me.r, me.col(y=d)))
        yield
        total = u2[b, rows(me.y, 64)]
        for d in range(1, 4):
            links.arrived(ns[d - 1], ybuf.at[b, d - 1], (me.r, me.col(y=d)))
            total = total + ybuf[b, d - 1]
        tbuf[b] = total.reshape(4, 16, 512)
        ns = [links.new() for _ in range(3)]
        for d in range(1, 4):
            links.go(ns[d - 1], tbuf.at[b, (me.h + d) % 4], hbuf.at[b, d - 1], (me.r, me.col(h=d)))
        yield
        total = tbuf[b, me.h]
        for d in range(1, 4):
            links.arrived(ns[d - 1], hbuf.at[b, d - 1], (me.r, me.col(h=d)))
            total = total + hbuf[b, d - 1]
        source = src[rows(b * 16 + me.c, 16), :].astype(F32)
        high, low = split((0.5 * source + total) / pre[0])
        both[pl.ds(b * 16, 16)] = high
        both[pl.ds(32 + b * 16, 16)] = low
        yield

    chains = [chain(b) for b in HALVES]
    for b in (0, 1, 0, 1, 0, 1):
        next(chains[b])

    def third(ref, k):
        for j in range(8):
            product = nt(both[...], al[:, j * 2 + k].reshape(256, 512))
            ref[j] = product[:32] + product[32:]

    third(kp, other)
    waiting = swap(kp, kx)
    third(ko, me.k)
    waiting()
    ko[...] += kx[...]
    ns = [links.new() for _ in PEERS]
    for n, (dz, dx) in enumerate(PEERS):
        links.go(ns[n], ko.at[peer_j(dz, dx)], kbuf.at[n], (me.row(zl=dz, x=dx), me.c))
    total = ko[me.j]
    for n, (dz, dx) in enumerate(PEERS):
        links.arrived(ns[n], kbuf.at[n], (me.row(zl=dz, x=dx), me.c))
        total = total + kbuf[n]
    turned = total.T.reshape(16, 4, 4, 32)
    kt[...] = jnp.concatenate([turned[:, g] for g in range(4)], axis=-1)
    fin[me.c] = kt[me.c]
    ns = [links.new() for _ in range(16)]
    for d in range(1, 16):
        to = (me.c + d) % 16
        links.go(ns[d], kt.at[to], fin.at[me.c], (me.r, to))
    lanes = line(weights, me.c, 2).astype(F32) * power(line(exps, me.c, 2), 2.0, 0.5)
    mask = iota((16, 256), 1) == iota((16, 256), 0) + me.r * 16
    weight = jnp.sum(jnp.where(mask, lanes, 0.0), axis=1, keepdims=True) / math.sqrt(NG)
    for d in range(1, 16):
        links.arrived(ns[d], fin.at[(me.c - d) % 16], (me.r, (me.c + d) % 16))
    packed = [fin[n] for n in range(16)]
    gathered = [
        jnp.concatenate([one[:, g * 32 : g * 32 + 32] for one in packed], axis=1) for g in range(4)
    ]
    kernel[...] = jnp.concatenate(gathered, axis=0) * weight
    finish()


def crossed_back(row, col):
    return number(
        bit(row, 3) + bit(col, 3), bit(row, 2) + bit(col, 2),
        bit(row, 0) + bit(col, 0), bit(row, 1) + bit(col, 1),
    )


def screen(density, exps, weights, ids, shift, background, stop=99):
    def body(*refs):
        screen_kernel(stop, *refs)

    dma = pltpu.SemaphoreType.DMA
    vmem = pltpu.VMEM
    inside = pl.BlockSpec(memory_space=pltpu.VMEM)
    outside = pl.BlockSpec(memory_space=pl.ANY)
    return pl.pallas_call(
        body,
        out_shape=(
            jax.ShapeDtypeStruct((512, 512), F32),
            jax.ShapeDtypeStruct((16, NRES), F32),
        ),
        in_specs=[inside] * 5 + [outside],
        out_specs=(outside, inside),
        scratch_shapes=[
            vmem((16, 16, 16, 512), BF), vmem((16, 16, 16, 512), BF), vmem((16, 16, 512), BF),
            vmem((512, 512), F32), vmem((512, 512), F32), vmem((512, 512), BF), vmem((512, 512), BF),
            vmem((512, 512), F32), vmem((32, 512), F32), vmem((512, 512), BF), vmem((2, 512, 512), BF),
            vmem((512, 128), jnp.int32), vmem((2, 1, 512), F32),
            vmem((2, 512, 256), F32), vmem((2, 256, 256), F32), vmem((2, 8, 32, 256), F32),
            vmem((2, 7, 32, 256), F32), vmem((2, 16, 2, 32, 256), BF), vmem((2, 256, 512), F32),
            vmem((2, 3, 64, 512), F32), vmem((2, 4, 16, 512), F32), vmem((2, 3, 16, 512), F32),
            vmem((64, 512), BF),
            vmem((8, 32, 256), F32), vmem((8, 32, 256), F32), vmem((8, 32, 256), F32),
            vmem((7, 32, 256), F32), vmem((16, 4, 128), F32), vmem((16, 4, 128), F32),
            dma((NSEM,)), dma((NSEM,)), dma((2,)),
        ],
        compiler_params=pltpu.CompilerParams(
            collective_id=0, has_side_effects=True, vmem_limit_bytes=56 << 20
        ),
        name="screen",
    )(density, exps, weights, ids, shift, background)


def shards(pair_density, scale_exp, pair_weight, resident_ids, diagonal_shift, background):
    return screen(
        pair_density, scale_exp.reshape(32, 128), pair_weight.reshape(32, 128),
        resident_ids.reshape(4, 128), diagonal_shift.reshape(64, 128), background,
    )


def solution(mesh):
    return jax.shard_map(
        shards,
        mesh=mesh,
        in_specs=(P("col", "row"), P(), P(), P(), P(), P("row", "col")),
        out_specs=(P("row", "col"), P(("col", "row"), None)),
        check_vma=False,
    )
```

```python
import math

import jax
import jax.numpy as jnp
from jax import lax
from jax.experimental import pallas as pl
from jax.experimental.pallas import tpu as pltpu
from jax.sharding import PartitionSpec as P

NG = 8192
NRES = 512
NPAIR = 4096
MESH = pl.DeviceIdType.MESH
BF = jnp.bfloat16
F32 = jnp.float32
NSEM = 192


def bit(n, at):
    return (n // 2**at) % 2


def number(b3, b2, b1, b0):
    return (b3 % 2) * 8 + (b2 % 2) * 4 + (b1 % 2) * 2 + b0 % 2


def crossed(row, col):
    return number(
        bit(row, 3) + bit(col, 3), bit(row, 2) + bit(col, 2),
        bit(row, 0) + bit(col, 1), bit(row, 1) + bit(col, 0),
    )


class Place:
    def __init__(self):
        self.r = lax.axis_index("row")
        self.c = lax.axis_index("col")
        self.zl = self.r // 8
        self.x = (self.r // 2) % 4
        self.k = self.r % 2
        self.y = self.c // 4
        self.h = self.c % 4
        self.j = self.r // 2

    def row(self, zl=0, x=0, k=0):
        return ((self.zl + zl) % 2) * 8 + ((self.x + x) % 4) * 2 + (self.k + k) % 2

    def col(self, y=0, h=0):
        return ((self.y + y) % 4) * 4 + (self.h + h) % 4


class Links:
    def __init__(self, send, recv):
        self.send, self.recv, self.used, self.sent = send, recv, 0, []

    def new(self):
        self.used += 1
        return self.used - 1

    def copy(self, n, src, dst, to):
        return pltpu.make_async_remote_copy(
            src_ref=src, dst_ref=dst, send_sem=self.send.at[n], recv_sem=self.recv.at[n],
            device_id=to, device_id_type=MESH,
        )

    def go(self, n, src, dst, to):
        one = self.copy(n, src, dst, to)
        one.start()
        self.sent.append(one)

    def arrived(self, n, ref, to):
        self.copy(n, ref, ref, to).wait_recv()

    def drain(self):
        for one in self.sent:
            one.wait_send()
        self.sent = []


class Ring:
    def __init__(self, links, slots, step):
        self.links, self.slots, self.step = links, slots, step
        self.n = [links.new() for _ in range(4)]

    def start(self):
        for n, d in ((0, 1), (1, -1)):
            self.links.go(self.n[n], self.slots(0), self.slots(0), self.step(d))

    def half(self, d, n):
        size = self.slots(0).shape[0] // 2
        return self.slots(d).at[pl.ds(n * size, size)]

    def forward(self):
        for n, d in ((0, 1), (1, -1)):
            self.links.arrived(self.n[n], self.slots(-d), self.step(d))
            self.links.go(self.n[2 + n], self.half(-d, n), self.half(-d, n), self.step(d))

    def last(self):
        for n, d in ((0, 1), (1, -1)):
            self.links.arrived(self.n[2 + n], self.half(-2 * d, n), self.step(d))


def split(value):
    high = value.astype(BF)
    return high, (value - high.astype(F32)).astype(BF)


def nn(a, b):
    return lax.dot_general(a, b, (((1,), (0,)), ((), ())), preferred_element_type=F32)


def nt(a, b):
    return lax.dot_general(a, b, (((1,), (1,)), ((), ())), preferred_element_type=F32)


def tn(a, b):
    return lax.dot_general(a, b, (((0,), (0,)), ((), ())), preferred_element_type=F32)


def rows(start, size):
    return pl.ds(pl.multiple_of(start * size, size), size)


def iota(shape, axis):
    return lax.broadcasted_iota(jnp.int32, shape, axis)


def line(ref, start, count):
    return jnp.concatenate([ref[pl.ds(start * count + n, 1), :] for n in range(count)], axis=1)


def power(exponent, down=0.5, up=2.0):
    return jnp.where(exponent < 0, down, jnp.where(exponent > 0, up, 1.0)).astype(F32)


PEERS = [(a, b) for a in range(2) for b in range(4) if (a, b) != (0, 0)]
HALVES = range(2)


def screen_kernel(
    stop, density, exps, weights, ids, shift, background, dielectric, kernel,
    al, ar, hop, bg, dv, dh, dl, acc, acc_c, src, s0, idc, pre,
    u1, xbuf, wbuf, rbuf, s1, u2, ybuf, tbuf, hbuf, both, kp, kx, ko, kbuf, kt, fin,
    send, recv, local,
):
    me = Place()
    links = Links(send, recv)
    barrier = pltpu.get_barrier_semaphore()
    comes_from = (crossed(me.r, me.c), me.c)
    goes_to = (crossed_back(me.r, me.c), me.c)
    second = (me.r, crossed(me.r, me.c))
    neighbours = [
        (me.row(k=1), me.c), (me.row(x=1), me.c), (me.row(x=-1), me.c), (me.row(zl=1), me.c),
        (me.r, me.col(y=1)), (me.r, me.col(y=-1)), (me.r, me.col(h=1)), (me.r, me.col(h=-1)),
    ]
    for to in neighbours:
        pl.semaphore_signal(barrier, inc=1, device_id=to, device_id_type=MESH)

    @pl.when(comes_from[0] != me.r)
    def _():
        pl.semaphore_signal(barrier, inc=1, device_id=comes_from, device_id_type=MESH)

    @pl.when(second[1] != me.c)
    def _():
        pl.semaphore_signal(barrier, inc=1, device_id=second, device_id_type=MESH)

    expected = len(neighbours) + jnp.where(goes_to[0] != me.r, 1, 0) + jnp.where(second[1] != me.c, 1, 0)
    bg_in = pltpu.make_async_copy(background, bg, local.at[0])
    bg_in.start()
    factors = line(exps, me.c, 2)
    on_diagonal = iota((256, 256), 0) == iota((256, 256), 1)
    column = jnp.sum(jnp.where(on_diagonal, power(factors), 0.0), axis=1, keepdims=True)
    own = (density[...].astype(F32) * column).astype(BF).reshape(16, 16, 512)
    al[me.c] = own
    pl.semaphore_wait(barrier, expected)

    def part(ref, slot, p):
        return ref.at[slot, pl.ds(p * 8, 8)]

    first_to = (crossed_back(me.r, me.c), me.c)
    second_to = (me.r, crossed(me.r, me.c))
    stays = first_to[0] == me.r

    def slot_of(row):
        return crossed(row, me.c)

    mine = slot_of(me.r)

    class Panel:
        def __init__(self, p):
            self.p = p
            self.hop1, self.hop2, self.low = links.new(), links.new(), links.new()
            self.rings = [
                Ring(links, lambda d, n=n: part(ar, slot_of(me.row(zl=n, x=d)), p),
                     lambda d: (me.row(x=d), me.c))
                for n in range(2)
            ]
            self.hands = []

        def copy1(self):
            return links.copy(self.hop1, part(al, me.c, self.p), hop.at[pl.ds(self.p * 8, 8)], first_to)

        def copy2(self):
            return links.copy(self.hop2, hop.at[pl.ds(self.p * 8, 8)], part(ar, me.c, self.p), second_to)

        def hand(self, n, d):
            at = links.new()
            ref = part(ar, slot_of(me.row(zl=n, x=d)), self.p)
            links.go(at, ref, ref, (me.row(k=1), me.c))
            self.hands.append((at, part(ar, slot_of(me.row(zl=n, x=d, k=1)), self.p)))

        def step1(self):
            @pl.when(jnp.logical_not(stays))
            def _():
                self.copy1().start()

            @pl.when(stays)
            def _():
                hop[pl.ds(self.p * 8, 8)] = al[me.c, pl.ds(self.p * 8, 8)]

        def step2(self):
            here = hop.at[pl.ds(self.p * 8, 8)]

            @pl.when(jnp.logical_not(stays))
            def _():
                links.arrived(self.hop1, here, first_to)

            @pl.when(me.r != 0)
            def _():
                links.copy(self.hop2, here, part(ar, me.c, self.p), second_to).start()

            @pl.when(me.r == 0)
            def _():
                ar[mine, pl.ds(self.p * 8, 8)] = hop[pl.ds(self.p * 8, 8)]

        def step3(self):
            @pl.when(me.r != 0)
            def _():
                links.arrived(self.hop2, part(ar, mine, self.p), second_to)

            there = part(ar, mine, self.p)
            links.go(self.low, there, there, (me.row(zl=1), me.c))
            self.rings[0].start()
            self.hand(0, 0)

        def step4(self):
            links.arrived(self.low, part(ar, slot_of(me.row(zl=1)), self.p), (me.row(zl=1), me.c))
            self.rings[1].start()
            self.hand(1, 0)

        def forward(self, n):
            self.rings[n].forward()
            self.hand(n, 1)
            self.hand(n, -1)

        def last(self, n):
            self.rings[n].last()
            self.hand(n, 2)

        def end(self):
            for at, ref in self.hands:
                links.arrived(at, ref, (me.row(k=1), me.c))

        def drain(self):
            @pl.when(jnp.logical_not(stays))
            def _():
                self.copy1().wait_send()

            @pl.when(me.r != 0)
            def _():
                self.copy2().wait_send()

    panel = [Panel(p) for p in range(2)]
    zz = [
        Ring(links, lambda d, p=p: part(al, me.col(h=d), p), lambda d: (me.r, me.col(h=d)))
        for p in range(2)
    ]
    yy = [
        [
            Ring(links, lambda d, p=p, o=o: part(al, me.col(y=d, h=o), p),
                 lambda d: (me.r, me.col(y=d)))
            for o in (0, -1, 1, 2)
        ]
        for p in range(2)
    ]
    panel[0].step1()
    panel[1].step1()
    zz[0].start()
    yy[0][0].start()
    zz[1].start()
    yy[1][0].start()

    to_lane = iota((512, 512), 0)
    to_lane = (to_lane % 256) // 16 * 32 + to_lane // 256 * 16 + to_lane % 16
    wanted = jnp.where(to_lane == iota((512, 512), 1), line(ids, 0, 4), 0)
    idc[...] = jnp.broadcast_to(jnp.sum(wanted, axis=1, keepdims=True), (512, 128))
    acc[...] = jnp.zeros((512, 512), F32)
    pre[...] = jnp.zeros((2, 1, 512), F32)

    def picks(id_column, slot):
        count = id_column.shape[0]
        inverse = power(line(exps, slot, 2), 2.0, 0.5)
        hit = id_column == iota((count, 256), 1) + slot * 256
        return jnp.where(hit, inverse, 0.0).astype(BF)

    def squares(n, ref, slot):
        wide = ref[slot].reshape(256, 512).astype(F32)
        pre[n] += jnp.sum(wide * wide, axis=0, keepdims=True)

    def take(slot):
        squares(0, al, slot)
        acc[...] += nn(picks(idc[:, :1], slot), al[slot].reshape(256, 512))

    q = me.k * 8 + me.j
    own_ids = jnp.concatenate([idc[rows(q, 16), :], idc[rows(16 + q, 16), :]], axis=0)[:, :1]
    acc_c[...] = jnp.zeros((32, 512), F32)

    def take_right(slot):
        squares(1, ar, slot)
        acc_c[...] += nn(picks(own_ids, slot), ar[slot].reshape(256, 512))

    panel[0].step2()
    yy[0][0].forward()
    panel[1].step2()
    yy[1][0].forward()
    zz[0].forward()
    yy[0][1].start()
    yy[0][2].start()
    take(me.c)
    panel[0].step3()
    zz[1].forward()
    yy[1][1].start()
    yy[1][2].start()
    panel[0].step4()
    panel[1].step3()
    zz[0].last()
    yy[0][3].start()
    panel[1].step4()
    panel[0].forward(0)
    zz[1].last()
    yy[1][3].start()
    take(me.col(h=1))
    take(me.col(h=-1))
    yy[0][1].forward()
    yy[0][2].forward()
    panel[0].forward(1)
    panel[1].forward(0)
    yy[1][1].forward()
    yy[1][2].forward()
    panel[0].last(0)
    panel[1].forward(1)
    take(me.col(h=2))
    take(me.col(y=1))
    take(me.col(y=-1))
    panel[0].last(1)
    yy[0][3].forward()
    panel[1].last(0)
    for n in range(2):
        for d in (0, 1, -1):
            take_right(slot_of(me.row(zl=n, x=d)))
    panel[1].last(1)
    yy[1][3].forward()
    take_right(slot_of(me.row(x=2)))
    take_right(slot_of(me.row(zl=1, x=2)))
    for o in (-1, 1, 2):
        take(me.col(y=1, h=o))
        take(me.col(y=-1, h=o))
    for n, o in enumerate((0, -1, 1, 2)):
        yy[0][n].last()
        yy[1][n].last()
        take(me.col(y=2, h=o))
    for one in panel:
        one.end()

    scale = 1.0 / (4 * NPAIR)
    shift_row = line(shift, me.r, 4)
    precond = shift_row + pre[0] * scale
    pre[0] = precond
    src[...] = acc[...].astype(BF)
    high, low = split(acc[...] / precond)
    s0[0] = high
    s0[1] = low
    bg_in.wait()
    diagonal = (iota((512, 512), 0) == iota((512, 512), 1)) & (me.r == me.c)
    response = tn(al[...].reshape(NPAIR, 512), ar[...].reshape(NPAIR, 512)) * scale
    value = bg[...] + response + jnp.where(diagonal, shift_row, 0.0)
    dv[...] = value
    high, low = split(jnp.where(diagonal, precond, 0.0) - 0.5 * value)
    dh[...] = high
    dl[...] = low
    d_out = pltpu.make_async_copy(dv, dielectric, local.at[1])
    d_out.start()

    def finish():
        links.drain()
        for one in panel:
            one.drain()
        d_out.wait()

    if stop == 0:
        kernel[...] = dv[:16, :]
        finish()
        return

    other = 1 - me.k

    def peer_j(a, b):
        return ((me.zl + a) % 2) * 4 + (me.x + b) % 4

    def swap(src_ref, dst_ref):
        at = links.new()
        links.go(at, src_ref, dst_ref, (me.row(k=1), me.c))
        return lambda: links.arrived(at, dst_ref, (me.row(k=1), me.c))

    def chain(b):
        at = pl.ds(b * 256, 256)
        u1[b] = nn(s0[0, at], dh[...]) + nn(s0[0, at], dl[...]) + nn(s0[1, at], dh[...])
        waiting = swap(u1.at[b, rows(other, 128)], xbuf.at[b])
        yield 1
        waiting()
        wbuf[b] = (u1[b, rows(me.k, 128)] + xbuf[b]).reshape(8, 16, 512)
        ns = [links.new() for _ in PEERS]
        for n, (dz, dx) in enumerate(PEERS):
            links.go(ns[n], wbuf.at[b, peer_j(dz, dx)], rbuf.at[b, n], (me.row(zl=dz, x=dx), me.c))
        if b == 0:
            for n in range(2):
                for d in range(4):
                    take_right(slot_of(me.row(zl=n, x=d, k=1)))
            pre[1] = line(shift, me.c, 4) + pre[1] * scale
        yield 2
        total = wbuf[b, me.j]
        for n, (dz, dx) in enumerate(PEERS):
            links.arrived(ns[n], rbuf.at[b, n], (me.row(zl=dz, x=dx), me.c))
            total = total + rbuf[b, n]
        high, low = split((0.5 * acc_c[pl.ds(b * 16, 16), :] + total) / pre[1])
        s1[b, q, 0] = high
        s1[b, q, 1] = low
        ns = [links.new() for _ in PEERS]
        for n, (dz, dx) in enumerate(PEERS):
            links.go(ns[n], s1.at[b, q], s1.at[b, q], (me.row(zl=dz, x=dx), me.c))
        hands = []

        def hand(j):
            n = links.new()
            links.go(n, s1.at[b, me.k * 8 + j], s1.at[b, me.k * 8 + j], (me.row(k=1), me.c))
            hands.append((n, s1.at[b, other * 8 + j]))

        hand(me.j)
        yield 3
        for n, (dz, dx) in enumerate(PEERS):
            j = peer_j(-dz, -dx)
            links.arrived(ns[n], s1.at[b, me.k * 8 + j], (me.row(zl=dz, x=dx), me.c))
            hand(j)
        yield 4
        for n, ref in hands:
            links.arrived(n, ref, (me.row(k=1), me.c))
        high = s1[b, :, 0].reshape(256, 512)
        low = s1[b, :, 1].reshape(256, 512)
        u2[b] = nt(high, dh[...]) + nt(high, dl[...]) + nt(low, dh[...])
        ns = [links.new() for _ in range(3)]
        for d in range(1, 4):
            links.go(ns[d - 1], u2.at[b, rows((me.y + d) % 4, 64)], ybuf.at[b, d - 1],
                     (me.r, me.col(y=d)))
        yield 5
        total = u2[b, rows(me.y, 64)]
        for d in range(1, 4):
            links.arrived(ns[d - 1], ybuf.at[b, d - 1], (me.r, me.col(y=d)))
            total = total + ybuf[b, d - 1]
        tbuf[b] = total.reshape(4, 16, 512)
        ns = [links.new() for _ in range(3)]
        for d in range(1, 4):
            links.go(ns[d - 1], tbuf.at[b, (me.h + d) % 4], hbuf.at[b, d - 1], (me.r, me.col(h=d)))
        yield 6
        total = tbuf[b, me.h]
        for d in range(1, 4):
            links.arrived(ns[d - 1], hbuf.at[b, d - 1], (me.r, me.col(h=d)))
            total = total + hbuf[b, d - 1]
        source = src[rows(b * 16 + me.c, 16), :].astype(F32)
        high, low = split((0.5 * source + total) / pre[0])
        both[pl.ds(b * 16, 16)] = high
        both[pl.ds(32 + b * 16, 16)] = low
        yield 7

    chains = [chain(b) for b in HALVES]
    for step in range(9):
        for b in HALVES:
            if 1 <= step - b + 1 <= 7 and step - b + 1 <= stop:
                next(chains[b])
    if stop < 8:
        kernel[...] = dv[:16, :]
        finish()
        return

    def third(ref, k):
        for j in range(8):
            product = nt(both[...], al[:, j * 2 + k].reshape(256, 512))
            ref[j] = product[:32] + product[32:]

    third(kp, other)
    waiting = swap(kp, kx)
    third(ko, me.k)
    waiting()
    ko[...] += kx[...]
    ns = [links.new() for _ in PEERS]
    for n, (dz, dx) in enumerate(PEERS):
        links.go(ns[n], ko.at[peer_j(dz, dx)], kbuf.at[n], (me.row(zl=dz, x=dx), me.c))
    total = ko[me.j]
    for n, (dz, dx) in enumerate(PEERS):
        links.arrived(ns[n], kbuf.at[n], (me.row(zl=dz, x=dx), me.c))
        total = total + kbuf[n]
    if stop == 8:
        kernel[...] = dv[:16, :]
        finish()
        return
    turned = total.T.reshape(16, 4, 4, 32)
    kt[...] = jnp.concatenate([turned[:, g] for g in range(4)], axis=-1)
    fin[me.c] = kt[me.c]
    ns = [links.new() for _ in range(16)]
    for d in range(1, 16):
        to = (me.c + d) % 16
        links.go(ns[d], kt.at[to], fin.at[me.c], (me.r, to))
    lanes = line(weights, me.c, 2).astype(F32) * power(line(exps, me.c, 2), 2.0, 0.5)
    mask = iota((16, 256), 1) == iota((16, 256), 0) + me.r * 16
    weight = jnp.sum(jnp.where(mask, lanes, 0.0), axis=1, keepdims=True) / math.sqrt(NG)
    for d in range(1, 16):
        links.arrived(ns[d], fin.at[(me.c - d) % 16], (me.r, (me.c + d) % 16))
    packed = [fin[n] for n in range(16)]
    gathered = [
        jnp.concatenate([one[:, g * 32 : g * 32 + 32] for one in packed], axis=1) for g in range(4)
    ]
    kernel[...] = jnp.concatenate(gathered, axis=0) * weight
    finish()


def crossed_back(row, col):
    return number(
        bit(row, 3) + bit(col, 3), bit(row, 2) + bit(col, 2),
        bit(row, 0) + bit(col, 0), bit(row, 1) + bit(col, 1),
    )


def screen(density, exps, weights, ids, shift, background, stop=99):
    def body(*refs):
        screen_kernel(stop, *refs)

    dma = pltpu.SemaphoreType.DMA
    vmem = pltpu.VMEM
    inside = pl.BlockSpec(memory_space=pltpu.VMEM)
    outside = pl.BlockSpec(memory_space=pl.ANY)
    return pl.pallas_call(
        body,
        out_shape=(
            jax.ShapeDtypeStruct((512, 512), F32),
            jax.ShapeDtypeStruct((16, NRES), F32),
        ),
        in_specs=[inside] * 5 + [outside],
        out_specs=(outside, inside),
        scratch_shapes=[
            vmem((16, 16, 16, 512), BF), vmem((16, 16, 16, 512), BF), vmem((16, 16, 512), BF),
            vmem((512, 512), F32), vmem((512, 512), F32), vmem((512, 512), BF), vmem((512, 512), BF),
            vmem((512, 512), F32), vmem((32, 512), F32), vmem((512, 512), BF), vmem((2, 512, 512), BF),
            vmem((512, 128), jnp.int32), vmem((2, 1, 512), F32),
            vmem((2, 256, 512), F32), vmem((2, 128, 512), F32), vmem((2, 8, 16, 512), F32),
            vmem((2, 7, 16, 512), F32), vmem((2, 16, 2, 16, 512), BF), vmem((2, 256, 512), F32),
            vmem((2, 3, 64, 512), F32), vmem((2, 4, 16, 512), F32), vmem((2, 3, 16, 512), F32),
            vmem((64, 512), BF),
            vmem((8, 32, 256), F32), vmem((8, 32, 256), F32), vmem((8, 32, 256), F32),
            vmem((7, 32, 256), F32), vmem((16, 4, 128), F32), vmem((16, 4, 128), F32),
            dma((NSEM,)), dma((NSEM,)), dma((2,)),
        ],
        compiler_params=pltpu.CompilerParams(
            collective_id=0, has_side_effects=True, vmem_limit_bytes=56 << 20
        ),
        name="screen",
    )(density, exps, weights, ids, shift, background)


def shards(pair_density, scale_exp, pair_weight, resident_ids, diagonal_shift, background):
    return screen(
        pair_density, scale_exp.reshape(32, 128), pair_weight.reshape(32, 128),
        resident_ids.reshape(4, 128), diagonal_shift.reshape(64, 128), background,
    )


def solution(mesh):
    return jax.shard_map(
        shards,
        mesh=mesh,
        in_specs=(P("col", "row"), P(), P(), P(), P(), P("row", "col")),
        out_specs=(P("row", "col"), P(("col", "row"), None)),
        check_vma=False,
    )
```

```python
import math

import jax
import jax.numpy as jnp
from jax import lax
from jax.experimental import pallas as pl
from jax.experimental.pallas import tpu as pltpu
from jax.sharding import PartitionSpec as P

NG = 8192
NRES = 512
NPAIR = 4096
MESH = pl.DeviceIdType.MESH
BF = jnp.bfloat16
F32 = jnp.float32
NSEM = 192


def bit(n, at):
    return (n // 2**at) % 2


def number(b3, b2, b1, b0):
    return (b3 % 2) * 8 + (b2 % 2) * 4 + (b1 % 2) * 2 + b0 % 2


def crossed(row, col):
    return number(
        bit(row, 3) + bit(col, 3), bit(row, 2) + bit(col, 2),
        bit(row, 0) + bit(col, 1), bit(row, 1) + bit(col, 0),
    )


class Place:
    def __init__(self):
        self.r = lax.axis_index("row")
        self.c = lax.axis_index("col")
        self.zl = self.r // 8
        self.x = (self.r // 2) % 4
        self.k = self.r % 2
        self.y = self.c // 4
        self.h = self.c % 4
        self.j = self.r // 2

    def row(self, zl=0, x=0, k=0):
        return ((self.zl + zl) % 2) * 8 + ((self.x + x) % 4) * 2 + (self.k + k) % 2

    def col(self, y=0, h=0):
        return ((self.y + y) % 4) * 4 + (self.h + h) % 4


class Links:
    def __init__(self, send, recv):
        self.send, self.recv, self.used, self.sent = send, recv, 0, []

    def new(self):
        self.used += 1
        return self.used - 1

    def copy(self, n, src, dst, to):
        return pltpu.make_async_remote_copy(
            src_ref=src, dst_ref=dst, send_sem=self.send.at[n], recv_sem=self.recv.at[n],
            device_id=to, device_id_type=MESH,
        )

    def go(self, n, src, dst, to):
        one = self.copy(n, src, dst, to)
        one.start()
        self.sent.append(one)

    def arrived(self, n, ref, to):
        self.copy(n, ref, ref, to).wait_recv()

    def drain(self, count=None):
        count = len(self.sent) if count is None else count
        for one in self.sent[:count]:
            one.wait_send()
        self.sent = self.sent[count:]


class Ring:
    def __init__(self, links, slots, step):
        self.links, self.slots, self.step = links, slots, step
        self.n = [links.new() for _ in range(4)]

    def start(self):
        for n, d in ((0, 1), (1, -1)):
            self.links.go(self.n[n], self.slots(0), self.slots(0), self.step(d))

    def half(self, d, n):
        size = self.slots(0).shape[0] // 2
        return self.slots(d).at[pl.ds(n * size, size)]

    def forward(self):
        for n, d in ((0, 1), (1, -1)):
            self.links.arrived(self.n[n], self.slots(-d), self.step(d))
            self.links.go(self.n[2 + n], self.half(-d, n), self.half(-d, n), self.step(d))

    def last(self):
        for n, d in ((0, 1), (1, -1)):
            self.links.arrived(self.n[2 + n], self.half(-2 * d, n), self.step(d))


def split(value):
    high = value.astype(BF)
    return high, (value - high.astype(F32)).astype(BF)


def nn(a, b):
    return lax.dot_general(a, b, (((1,), (0,)), ((), ())), preferred_element_type=F32)


def nt(a, b):
    return lax.dot_general(a, b, (((1,), (1,)), ((), ())), preferred_element_type=F32)


def tn(a, b):
    return lax.dot_general(a, b, (((0,), (0,)), ((), ())), preferred_element_type=F32)


def rows(start, size):
    return pl.ds(pl.multiple_of(start * size, size), size)


def iota(shape, axis):
    return lax.broadcasted_iota(jnp.int32, shape, axis)


def line(ref, start, count):
    return jnp.concatenate([ref[pl.ds(start * count + n, 1), :] for n in range(count)], axis=1)


def power(exponent, down=0.5, up=2.0):
    return jnp.where(exponent < 0, down, jnp.where(exponent > 0, up, 1.0)).astype(F32)


PEERS = [(a, b) for a in range(2) for b in range(4) if (a, b) != (0, 0)]
HALVES = range(2)


def screen_kernel(
    stop, density, exps, weights, ids, shift, background, dielectric, kernel,
    al, ar, hop, bg, dv, dh, dl, acc, acc_c, src, s0, idc, pre,
    u1, xbuf, wbuf, rbuf, s1, u2, ybuf, tbuf, hbuf, both, kp, kx, ko, kbuf, kt, fin,
    send, recv, local,
):
    me = Place()
    links = Links(send, recv)
    barrier = pltpu.get_barrier_semaphore()
    comes_from = (crossed(me.r, me.c), me.c)
    goes_to = (crossed_back(me.r, me.c), me.c)
    second = (me.r, crossed(me.r, me.c))
    neighbours = [
        (me.row(k=1), me.c), (me.row(x=1), me.c), (me.row(x=-1), me.c), (me.row(zl=1), me.c),
        (me.r, me.col(y=1)), (me.r, me.col(y=-1)), (me.r, me.col(h=1)), (me.r, me.col(h=-1)),
    ]
    for to in neighbours:
        pl.semaphore_signal(barrier, inc=1, device_id=to, device_id_type=MESH)

    @pl.when(comes_from[0] != me.r)
    def _():
        pl.semaphore_signal(barrier, inc=1, device_id=comes_from, device_id_type=MESH)

    @pl.when(second[1] != me.c)
    def _():
        pl.semaphore_signal(barrier, inc=1, device_id=second, device_id_type=MESH)

    expected = len(neighbours) + jnp.where(goes_to[0] != me.r, 1, 0) + jnp.where(second[1] != me.c, 1, 0)
    bg_in = pltpu.make_async_copy(background, bg, local.at[0])
    bg_in.start()
    factors = line(exps, me.c, 2)
    on_diagonal = iota((256, 256), 0) == iota((256, 256), 1)
    column = jnp.sum(jnp.where(on_diagonal, power(factors), 0.0), axis=1, keepdims=True)
    own = (density[...].astype(F32) * column).astype(BF).reshape(16, 16, 512)
    al[me.c] = own
    pl.semaphore_wait(barrier, expected)

    def part(ref, slot, p):
        return ref.at[slot, pl.ds(p * 8, 8)]

    first_to = (crossed_back(me.r, me.c), me.c)
    second_to = (me.r, crossed(me.r, me.c))
    stays = first_to[0] == me.r

    def slot_of(row):
        return crossed(row, me.c)

    mine = slot_of(me.r)

    class Panel:
        def __init__(self, p):
            self.p = p
            self.hop1, self.hop2, self.low = links.new(), links.new(), links.new()
            self.rings = [
                Ring(links, lambda d, n=n: part(ar, slot_of(me.row(zl=n, x=d)), p),
                     lambda d: (me.row(x=d), me.c))
                for n in range(2)
            ]
            self.hands = []

        def copy1(self):
            return links.copy(self.hop1, part(al, me.c, self.p), hop.at[pl.ds(self.p * 8, 8)], first_to)

        def copy2(self):
            return links.copy(self.hop2, hop.at[pl.ds(self.p * 8, 8)], part(ar, me.c, self.p), second_to)

        def hand(self, n, d):
            at = links.new()
            ref = part(ar, slot_of(me.row(zl=n, x=d)), self.p)
            links.go(at, ref, ref, (me.row(k=1), me.c))
            self.hands.append((at, part(ar, slot_of(me.row(zl=n, x=d, k=1)), self.p)))

        def step1(self):
            @pl.when(jnp.logical_not(stays))
            def _():
                self.copy1().start()

            @pl.when(stays)
            def _():
                hop[pl.ds(self.p * 8, 8)] = al[me.c, pl.ds(self.p * 8, 8)]

        def step2(self):
            here = hop.at[pl.ds(self.p * 8, 8)]

            @pl.when(jnp.logical_not(stays))
            def _():
                links.arrived(self.hop1, here, first_to)

            @pl.when(me.r != 0)
            def _():
                links.copy(self.hop2, here, part(ar, me.c, self.p), second_to).start()

            @pl.when(me.r == 0)
            def _():
                ar[mine, pl.ds(self.p * 8, 8)] = hop[pl.ds(self.p * 8, 8)]

        def step3(self):
            @pl.when(me.r != 0)
            def _():
                links.arrived(self.hop2, part(ar, mine, self.p), second_to)

            there = part(ar, mine, self.p)
            links.go(self.low, there, there, (me.row(zl=1), me.c))
            self.rings[0].start()
            self.hand(0, 0)

        def step4(self):
            links.arrived(self.low, part(ar, slot_of(me.row(zl=1)), self.p), (me.row(zl=1), me.c))
            self.rings[1].start()
            self.hand(1, 0)

        def forward(self, n):
            self.rings[n].forward()
            self.hand(n, 1)
            self.hand(n, -1)

        def last(self, n):
            self.rings[n].last()
            self.hand(n, 2)

        def end(self):
            for at, ref in self.hands:
                links.arrived(at, ref, (me.row(k=1), me.c))

        def drain(self):
            @pl.when(jnp.logical_not(stays))
            def _():
                self.copy1().wait_send()

            @pl.when(me.r != 0)
            def _():
                self.copy2().wait_send()

    panel = [Panel(p) for p in range(2)]
    zz = [
        Ring(links, lambda d, p=p: part(al, me.col(h=d), p), lambda d: (me.r, me.col(h=d)))
        for p in range(2)
    ]
    yy = [
        [
            Ring(links, lambda d, p=p, o=o: part(al, me.col(y=d, h=o), p),
                 lambda d: (me.r, me.col(y=d)))
            for o in (0, -1, 1, 2)
        ]
        for p in range(2)
    ]
    panel[0].step1()
    panel[1].step1()
    zz[0].start()
    yy[0][0].start()
    zz[1].start()
    yy[1][0].start()

    to_lane = iota((512, 512), 0)
    to_lane = (to_lane % 256) // 16 * 32 + to_lane // 256 * 16 + to_lane % 16
    wanted = jnp.where(to_lane == iota((512, 512), 1), line(ids, 0, 4), 0)
    idc[...] = jnp.broadcast_to(jnp.sum(wanted, axis=1, keepdims=True), (512, 128))
    acc[...] = jnp.zeros((512, 512), F32)
    pre[...] = jnp.zeros((2, 1, 512), F32)

    def picks(id_column, slot):
        count = id_column.shape[0]
        inverse = power(line(exps, slot, 2), 2.0, 0.5)
        hit = id_column == iota((count, 256), 1) + slot * 256
        return jnp.where(hit, inverse, 0.0).astype(BF)

    def squares(n, ref, slot):
        wide = ref[slot].reshape(256, 512).astype(F32)
        pre[n] += jnp.sum(wide * wide, axis=0, keepdims=True)

    def take(slot):
        squares(0, al, slot)
        acc[...] += nn(picks(idc[:, :1], slot), al[slot].reshape(256, 512))

    q = me.k * 8 + me.j
    own_ids = jnp.concatenate([idc[rows(q, 16), :], idc[rows(16 + q, 16), :]], axis=0)[:, :1]
    acc_c[...] = jnp.zeros((32, 512), F32)

    def take_right(slot):
        squares(1, ar, slot)
        acc_c[...] += nn(picks(own_ids, slot), ar[slot].reshape(256, 512))

    panel[0].step2()
    yy[0][0].forward()
    panel[1].step2()
    yy[1][0].forward()
    zz[0].forward()
    yy[0][1].start()
    yy[0][2].start()
    take(me.c)
    panel[0].step3()
    zz[1].forward()
    yy[1][1].start()
    yy[1][2].start()
    panel[0].step4()
    panel[1].step3()
    zz[0].last()
    yy[0][3].start()
    panel[1].step4()
    panel[0].forward(0)
    zz[1].last()
    yy[1][3].start()
    take(me.col(h=1))
    take(me.col(h=-1))
    yy[0][1].forward()
    yy[0][2].forward()
    panel[0].forward(1)
    panel[1].forward(0)
    yy[1][1].forward()
    yy[1][2].forward()
    panel[0].last(0)
    panel[1].forward(1)
    take(me.col(h=2))
    take(me.col(y=1))
    take(me.col(y=-1))
    panel[0].last(1)
    yy[0][3].forward()
    panel[1].last(0)
    for n in range(2):
        for d in (0, 1, -1):
            take_right(slot_of(me.row(zl=n, x=d)))
    panel[1].last(1)
    yy[1][3].forward()
    take_right(slot_of(me.row(x=2)))
    take_right(slot_of(me.row(zl=1, x=2)))
    for o in (-1, 1, 2):
        take(me.col(y=1, h=o))
        take(me.col(y=-1, h=o))
    for n, o in enumerate((0, -1, 1, 2)):
        yy[0][n].last()
        yy[1][n].last()
        take(me.col(y=2, h=o))
    for one in panel:
        one.end()

    scale = 1.0 / (4 * NPAIR)
    shift_row = line(shift, me.r, 4)
    precond = shift_row + pre[0] * scale
    pre[0] = precond
    src[...] = acc[...].astype(BF)
    high, low = split(acc[...] / precond)
    s0[0] = high
    s0[1] = low
    bg_in.wait()
    diagonal = (iota((512, 512), 0) == iota((512, 512), 1)) & (me.r == me.c)
    response = tn(al[...].reshape(NPAIR, 512), ar[...].reshape(NPAIR, 512)) * scale
    value = bg[...] + response + jnp.where(diagonal, shift_row, 0.0)
    dv[...] = value
    high, low = split(jnp.where(diagonal, precond, 0.0) - 0.5 * value)
    dh[...] = high
    dl[...] = low
    d_out = pltpu.make_async_copy(dv, dielectric, local.at[1])
    d_out.start()

    of_panels = len(links.sent)

    def finish():
        links.drain()
        if stop == 0:
            for one in panel:
                one.drain()
            d_out.wait()

    if stop == 0:
        kernel[...] = dv[:16, :]
        finish()
        return

    other = 1 - me.k

    def peer_j(a, b):
        return ((me.zl + a) % 2) * 4 + (me.x + b) % 4

    def swap(src_ref, dst_ref):
        at = links.new()
        links.go(at, src_ref, dst_ref, (me.row(k=1), me.c))
        return lambda: links.arrived(at, dst_ref, (me.row(k=1), me.c))

    sums = [links.new() for _ in PEERS]

    def chain(b):
        at = pl.ds(b * 256, 256)
        u1[b] = nn(s0[0, at], dh[...]) + nn(s0[0, at], dl[...]) + nn(s0[1, at], dh[...])
        waiting = swap(u1.at[b, rows(other, 128)], xbuf.at[b])
        yield 1
        waiting()
        wbuf[:, b] = (u1[b, rows(me.k, 128)] + xbuf[b]).reshape(8, 16, 512)
        if b == 1:
            for n, (dz, dx) in enumerate(PEERS):
                links.go(sums[n], wbuf.at[peer_j(dz, dx)], rbuf.at[n], (me.row(zl=dz, x=dx), me.c))
        if b == 1:
            for n in range(2):
                for d in range(4):
                    take_right(slot_of(me.row(zl=n, x=d, k=1)))
            pre[1] = line(shift, me.c, 4) + pre[1] * scale
            links.drain(of_panels)
            for one in panel:
                one.drain()
        yield 2
        total = wbuf[me.j, b]
        for n, (dz, dx) in enumerate(PEERS):
            if b == 0:
                links.arrived(sums[n], rbuf.at[n], (me.row(zl=dz, x=dx), me.c))
            total = total + rbuf[n, b]
        high, low = split((0.5 * acc_c[pl.ds(b * 16, 16), :] + total) / pre[1])
        s1[b, q, 0] = high
        s1[b, q, 1] = low
        ns = [links.new() for _ in PEERS]
        for n, (dz, dx) in enumerate(PEERS):
            links.go(ns[n], s1.at[b, q], s1.at[b, q], (me.row(zl=dz, x=dx), me.c))
        hands = []

        def hand(j):
            n = links.new()
            links.go(n, s1.at[b, me.k * 8 + j], s1.at[b, me.k * 8 + j], (me.row(k=1), me.c))
            hands.append((n, s1.at[b, other * 8 + j]))

        hand(me.j)
        yield 3
        for n, (dz, dx) in enumerate(PEERS):
            j = peer_j(-dz, -dx)
            links.arrived(ns[n], s1.at[b, me.k * 8 + j], (me.row(zl=dz, x=dx), me.c))
            hand(j)
        yield 4
        for n, ref in hands:
            links.arrived(n, ref, (me.row(k=1), me.c))
        high = s1[b, :, 0].reshape(256, 512)
        low = s1[b, :, 1].reshape(256, 512)
        u2[b] = nt(high, dh[...]) + nt(high, dl[...]) + nt(low, dh[...])
        ns = [links.new() for _ in range(3)]
        for d in range(1, 4):
            links.go(ns[d - 1], u2.at[b, rows((me.y + d) % 4, 64)], ybuf.at[b, d - 1],
                     (me.r, me.col(y=d)))
        yield 5
        total = u2[b, rows(me.y, 64)]
        for d in range(1, 4):
            links.arrived(ns[d - 1], ybuf.at[b, d - 1], (me.r, me.col(y=d)))
            total = total + ybuf[b, d - 1]
        tbuf[b] = total.reshape(4, 16, 512)
        ns = [links.new() for _ in range(3)]
        for d in range(1, 4):
            links.go(ns[d - 1], tbuf.at[b, (me.h + d) % 4], hbuf.at[b, d - 1], (me.r, me.col(h=d)))
        yield 6
        total = tbuf[b, me.h]
        for d in range(1, 4):
            links.arrived(ns[d - 1], hbuf.at[b, d - 1], (me.r, me.col(h=d)))
            total = total + hbuf[b, d - 1]
        source = src[rows(b * 16 + me.c, 16), :].astype(F32)
        high, low = split((0.5 * source + total) / pre[0])
        both[pl.ds(b * 16, 16)] = high
        both[pl.ds(32 + b * 16, 16)] = low
        yield 7

    chains = [chain(b) for b in HALVES]
    for b in (0, 1, 0, 1, 0, 1, 0, 0, 1, 1, 0, 1, 0, 1):
        next(chains[b])
    if stop < 8:
        kernel[...] = dv[:16, :]
        finish()
        return

    def third(ref, k):
        for j in range(8):
            product = nt(both[...], al[:, j * 2 + k].reshape(256, 512))
            ref[j] = product[:32] + product[32:]

    third(kp, other)
    waiting = swap(kp, kx)
    third(ko, me.k)
    waiting()
    ko[...] += kx[...]
    ns = [links.new() for _ in PEERS]
    for n, (dz, dx) in enumerate(PEERS):
        links.go(ns[n], ko.at[peer_j(dz, dx)], kbuf.at[n], (me.row(zl=dz, x=dx), me.c))
    total = ko[me.j]
    for n, (dz, dx) in enumerate(PEERS):
        links.arrived(ns[n], kbuf.at[n], (me.row(zl=dz, x=dx), me.c))
        total = total + kbuf[n]
    if stop == 8:
        kernel[...] = dv[:16, :]
        finish()
        return
    turned = total.T.reshape(16, 4, 4, 32)
    kt[...] = jnp.concatenate([turned[:, g] for g in range(4)], axis=-1)
    fin[me.c] = kt[me.c]
    before = len(links.sent)
    ns = [links.new() for _ in range(16)]
    for d in range(1, 16):
        to = (me.c + d) % 16
        links.go(ns[d], kt.at[to], fin.at[me.c], (me.r, to))
    links.drain(before)
    d_out.wait()
    lanes = line(weights, me.c, 2).astype(F32) * power(line(exps, me.c, 2), 2.0, 0.5)
    mask = iota((16, 256), 1) == iota((16, 256), 0) + me.r * 16
    weight = jnp.sum(jnp.where(mask, lanes, 0.0), axis=1, keepdims=True) / math.sqrt(NG)
    for d in range(1, 16):
        links.arrived(ns[d], fin.at[(me.c - d) % 16], (me.r, (me.c + d) % 16))
    packed = [fin[n] for n in range(16)]
    gathered = [
        jnp.concatenate([one[:, g * 32 : g * 32 + 32] for one in packed], axis=1) for g in range(4)
    ]
    kernel[...] = jnp.concatenate(gathered, axis=0) * weight
    finish()


def crossed_back(row, col):
    return number(
        bit(row, 3) + bit(col, 3), bit(row, 2) + bit(col, 2),
        bit(row, 0) + bit(col, 0), bit(row, 1) + bit(col, 1),
    )


def screen(density, exps, weights, ids, shift, background, stop=99):
    def body(*refs):
        screen_kernel(stop, *refs)

    dma = pltpu.SemaphoreType.DMA
    vmem = pltpu.VMEM
    inside = pl.BlockSpec(memory_space=pltpu.VMEM)
    outside = pl.BlockSpec(memory_space=pl.ANY)
    return pl.pallas_call(
        body,
        out_shape=(
            jax.ShapeDtypeStruct((512, 512), F32),
            jax.ShapeDtypeStruct((16, NRES), F32),
        ),
        in_specs=[inside] * 5 + [outside],
        out_specs=(outside, inside),
        scratch_shapes=[
            vmem((16, 16, 16, 512), BF), vmem((16, 16, 16, 512), BF), vmem((16, 16, 512), BF),
            vmem((512, 512), F32), vmem((512, 512), F32), vmem((512, 512), BF), vmem((512, 512), BF),
            vmem((512, 512), F32), vmem((32, 512), F32), vmem((512, 512), BF), vmem((2, 512, 512), BF),
            vmem((512, 128), jnp.int32), vmem((2, 1, 512), F32),
            vmem((2, 256, 512), F32), vmem((2, 128, 512), F32), vmem((8, 2, 16, 512), F32),
            vmem((7, 2, 16, 512), F32), vmem((2, 16, 2, 16, 512), BF), vmem((2, 256, 512), F32),
            vmem((2, 3, 64, 512), F32), vmem((2, 4, 16, 512), F32), vmem((2, 3, 16, 512), F32),
            vmem((64, 512), BF),
            vmem((8, 32, 256), F32), vmem((8, 32, 256), F32), vmem((8, 32, 256), F32),
            vmem((7, 32, 256), F32), vmem((16, 4, 128), F32), vmem((16, 4, 128), F32),
            dma((NSEM,)), dma((NSEM,)), dma((2,)),
        ],
        compiler_params=pltpu.CompilerParams(
            collective_id=0, has_side_effects=True, vmem_limit_bytes=56 << 20
        ),
        name="screen",
    )(density, exps, weights, ids, shift, background)


def shards(pair_density, scale_exp, pair_weight, resident_ids, diagonal_shift, background):
    return screen(
        pair_density, scale_exp.reshape(32, 128), pair_weight.reshape(32, 128),
        resident_ids.reshape(4, 128), diagonal_shift.reshape(64, 128), background,
    )


def solution(mesh):
    return jax.shard_map(
        shards,
        mesh=mesh,
        in_specs=(P("col", "row"), P(), P(), P(), P(), P("row", "col")),
        out_specs=(P("row", "col"), P(("col", "row"), None)),
        check_vma=False,
    )
```
